32 devices in a mesh: basis: 16 (over z, x, core), band: 2 (over y).
Axes of the slice: x: 2, y: 2, z: 4, core: 2. Of those that a mesh axis runs over, the one named last changes fastest.
Arguments:
- matching: bfloat16 [162, 40960], P(None, 'basis'), may hold values from -6 to 6
- vectors: bfloat16 [40960, 4096], P('basis', 'band'), may hold values from -0.03125 to 0.03125
- weights: float32 [4096], P('band'), may hold values from 4.8828126e-05 to 0.00048828125
- gaunt_index: int32 [3, 4096], replicated, may hold values from 0 to 80
- gaunt_value: float32 [4096], replicated, may hold values from -4 to 4
Outputs:
- density_matrix: float32 [162, 162], replicated
- density: float32 [4, 81], replicated
The draws below stay inside these ranges and needn't reach their ends.
All inputs are finite; a program needn't handle non-finite values.
Results may differ from the reference program's by a relative error of at most 0.0003.
Values sent between devices are 32-bit elements; how exact they have to be, the bound alone decides.
No kernel may reach another device: no remote copies, remote signals or barrier semaphores. Data moves between devices by JAX's collectives and lax.ppermute only.
A program may use at most 64 MiB of HBM per device.

```python
import math
import jax
import jax.numpy as jnp
from jax import lax

HARM = 81
CH = 162
NBASIS = 40960
BAND_DEV = 2048
NBANDS = 4096
NGAUNT = 4096


def touch_ends(values, key, smallest, high):
    spot = [jax.random.randint(jax.random.fold_in(key, axis), (), 0, length) for axis, length in enumerate(values.shape)]
    longest = values.shape.index(max(values.shape))
    next_to = spot[:longest] + [(spot[longest] + 1) % values.shape[longest]] + spot[longest + 1:]
    return values.at[tuple(spot)].set(smallest).at[tuple(next_to)].set(high)


def levels(rng, extent, split, smallest, largest):
    gain = 1.0
    for axis_at, shards_of in split:
        steps = jax.random.uniform(jax.random.fold_in(jax.random.fold_in(rng, 6), axis_at), (shards_of,), jnp.float32, smallest / len(split), largest / len(split))
        gain = gain * jnp.repeat(jnp.exp(steps), extent[axis_at] // shards_of).reshape((-1,) + (1,) * (len(extent) - 1 - axis_at))
    return gain


def centred(own_key, extent, scale, limit, split=(), kind=jnp.bfloat16):
    array = jax.random.normal(own_key, extent, jnp.float32) * scale
    if len(split) > 0:
        array = levels(own_key, extent, split, -0.22, 0.18) * array
    return jnp.clip(array, min=-limit, max=limit).astype(kind)


def setup_inputs(seed: int = 0) -> dict:
    key_of = jax.random.split(jax.random.key(seed), 6)
    return {
        "matching": centred(key_of[0], (CH, NBASIS), 1.0, 6.0, ((1, 16),)),
        "vectors": centred(key_of[1], (NBASIS, NBANDS), NBASIS ** -0.5, 0.03125, ((0, 16), (1, 2))),
        "weights": jnp.clip(jnp.exp(math.log(0.00048828125) - 2.3025851 * jax.random.uniform(key_of[2], (NBANDS,), jnp.float32) ** levels(key_of[2], (NBANDS,), ((0, 2),), -0.2, 0.2)), 4.882812572759576e-05, 0.00048828125),
        "gaunt_index": touch_ends(jax.random.randint(key_of[3], (3, NGAUNT), 0, HARM), jax.random.fold_in(key_of[3], 1), 0, HARM - 1).astype(jnp.int32),
        "gaunt_value": centred(key_of[4], (NGAUNT,), 0.3, 4.0, (), jnp.float32),
    }


def reference(matching, vectors, weights, gaunt_index, gaunt_value):
    blocks = NBANDS // BAND_DEV
    left = matching.astype(jnp.float32)

    def one_block(index):
        start = (index * BAND_DEV).astype(jnp.int32)
        piece = lax.dynamic_slice_in_dim(vectors, start, BAND_DEV, 1).astype(jnp.float32)
        coeffs = jnp.dot(left, piece, precision=lax.Precision.HIGHEST, preferred_element_type=jnp.float32)
        scaled = coeffs * lax.dynamic_slice_in_dim(weights, start, BAND_DEV, 0)[None, :]
        return jnp.dot(scaled, coeffs.T, precision=lax.Precision.HIGHEST, preferred_element_type=jnp.float32)

    terms = lax.map(one_block, jnp.arange(blocks, dtype=jnp.int32))
    density_matrix = jnp.sum(terms, axis=0)
    blocked = density_matrix.reshape(2, HARM, 2, HARM)
    picked = blocked[:, gaunt_index[0], :, gaunt_index[1]]
    values = picked.reshape(NGAUNT, 4) * gaunt_value[:, None]
    density = jax.ops.segment_sum(values, gaunt_index[2], num_segments=HARM)
    return density_matrix, density.T
```

```python
import functools

import jax
import jax.numpy as jnp
from jax import lax
from jax.experimental import pallas as pl
from jax.experimental.pallas import tpu as pltpu
from jax.sharding import PartitionSpec as P

BLOCK = 256


def weighted_pairs(coeffs, band_weights):
    scaled = coeffs * band_weights[None, :]
    return lax.dot_general(
        scaled,
        coeffs,
        (((1,), (1,)), ((), ())),
        precision=lax.Precision.HIGHEST,
        preferred_element_type=jnp.float32,
    )


def gaunt_density(density_matrix, gaunt_index, gaunt_value):
    harmonics = density_matrix.shape[0] // 2
    codes = jnp.arange(harmonics, dtype=jnp.int32)[:, None]
    first_table = (gaunt_index[0][None, :] == codes).astype(jnp.float32)
    second_table = (gaunt_index[1][None, :] == codes).astype(jnp.float32)
    target_table = (gaunt_index[2][None, :] == codes).astype(jnp.float32)
    collected = []
    for radial in range(2):
        for other in range(2):
            block = density_matrix[
                radial * harmonics : (radial + 1) * harmonics,
                other * harmonics : (other + 1) * harmonics,
            ]
            spread = jnp.dot(
                block,
                second_table,
                precision=lax.Precision.HIGHEST,
                preferred_element_type=jnp.float32,
            )
            picked = jnp.sum(spread * first_table, axis=0)
            collected.append(picked * gaunt_value)
    values = jnp.stack(collected)
    return lax.dot_general(
        values,
        target_table,
        (((1,), (1,)), ((), ())),
        precision=lax.Precision.HIGHEST,
        preferred_element_type=jnp.float32,
    )


def product_kernel(blocks, part_ref, matching_hbm, vectors_hbm, out_ref, matching, vectors, matching_sem, sems):
    start = part_ref[0] * (blocks * BLOCK)
    first = pltpu.make_async_copy(matching_hbm, matching, matching_sem)
    first.start()
    copies = []
    for at in range(blocks):
        columns = pl.ds(pl.multiple_of(start + at * BLOCK, BLOCK), BLOCK)
        copies.append(pltpu.make_async_copy(vectors_hbm.at[:, columns], vectors.at[at], sems.at[at]))
        copies[-1].start()
    first.wait()
    for at in range(blocks):
        copies[at].wait()
        out_ref[:, at * BLOCK : (at + 1) * BLOCK] = jnp.dot(
            matching[...], vectors[at], preferred_element_type=jnp.float32
        )


def product(matching, vectors, part, columns):
    channels, depth = matching.shape
    blocks = columns // BLOCK
    return pl.pallas_call(
        functools.partial(product_kernel, blocks),
        out_shape=jax.ShapeDtypeStruct((channels, columns), jnp.float32),
        in_specs=[
            pl.BlockSpec(memory_space=pltpu.SMEM),
            pl.BlockSpec(memory_space=pltpu.HBM),
            pl.BlockSpec(memory_space=pltpu.HBM),
        ],
        out_specs=pl.BlockSpec(memory_space=pltpu.VMEM),
        scratch_shapes=[
            pltpu.VMEM((channels, depth), matching.dtype),
            pltpu.VMEM((blocks, depth, BLOCK), vectors.dtype),
            pltpu.SemaphoreType.DMA,
            pltpu.SemaphoreType.DMA((blocks,)),
        ],
        compiler_params=pltpu.CompilerParams(vmem_limit_bytes=58 * 2**20),
        cost_estimate=pl.CostEstimate(
            flops=2 * channels * depth * columns,
            bytes_accessed=2 * depth * (columns + channels) + 4 * channels * columns,
            transcendentals=0,
        ),
        name="product",
    )(part.reshape(1), matching, vectors)


def plain_body(matching, vectors, weights, gaunt_index, gaunt_value):
    partial_value = jnp.dot(matching, vectors, preferred_element_type=jnp.float32)
    summed = lax.psum(partial_value, "basis")
    local_terms = weighted_pairs(summed, weights)
    density_matrix = lax.psum(local_terms, "band")
    return (density_matrix, gaunt_density(density_matrix, gaunt_index, gaunt_value))


def halves(block, bit):
    middle = block.shape[1] // 2
    low, high = block[:, :middle], block[:, middle:]
    return jnp.where(bit == 1, low, high), jnp.where(bit == 1, high, low)


def body(basis, band, matching, vectors, weights, gaunt_index, gaunt_value):
    index = lax.axis_index("basis")
    levels = basis.bit_length() - 1
    columns = vectors.shape[1]
    bits = [(index >> level) & 1 for level in range(levels)]
    own = functools.reduce(jnp.bitwise_xor, bits)

    def exchange(block, mask, band_mask=0):
        pairs = [
            (i * band + j, (i ^ mask) * band + (j ^ band_mask))
            for i in range(basis)
            for j in range(band)
        ]
        return lax.ppermute(block, ("basis", "band"), pairs)

    leaving = product(matching, vectors, 1 - own, columns // 2)
    arriving = exchange(leaving, 1)
    staying = product(matching, vectors, own, columns // 2)
    total = staying + arriving
    width = columns // 4
    sent_a, kept_a = halves(total[:, :width], bits[1])
    sent_b, kept_b = halves(total[:, width:], bits[2])
    come_a, come_b = exchange(sent_a, 3), exchange(sent_b, 5)
    sent_a, kept_a = halves(kept_a + come_a, bits[2])
    sent_b, kept_b = halves(kept_b + come_b, bits[1])
    come_a, come_b = exchange(sent_a, 5), exchange(sent_b, 3)
    block = jnp.concatenate([kept_a + come_a, kept_b + come_b], axis=1)
    width = columns // 16
    begin = own * (columns // 2)
    block_weights = jnp.concatenate(
        [
            lax.dynamic_slice_in_dim(weights, begin + (2 * bits[1] + bits[2]) * width, width),
            lax.dynamic_slice_in_dim(weights, begin + columns // 4 + (2 * bits[2] + bits[1]) * width, width),
        ]
    )
    for level in range(3, levels - 1):
        sent, kept = halves(block, bits[level])
        block = kept + exchange(sent, 1 | (1 << level))
        middle = block_weights.shape[0] // 2
        block_weights = jnp.where(bits[level] == 1, block_weights[middle:], block_weights[:middle])
    block = block + exchange(block, 1 | (1 << (levels - 1)))

    terms = weighted_pairs(block, block_weights)
    terms = terms + exchange(terms, 1)
    step = 1
    while step < band:
        terms = terms + exchange(terms, 1, step)
        step *= 2
    for level in range(1, levels - 1):
        terms = terms + exchange(terms, 1 | (1 << level))
    return (terms, gaunt_density(terms, gaunt_index, gaunt_value))


def solution(mesh):
    basis, band = mesh.shape["basis"], mesh.shape["band"]

    def choose(*arrays):
        columns = arrays[1].shape[1]
        powers = basis & (basis - 1) == 0 and band & (band - 1) == 0 and basis >= 16
        if powers and columns % (2 * BLOCK) == 0 and columns % (16 * 128) == 0:
            return body(basis, band, *arrays)
        return plain_body(*arrays)

    return jax.shard_map(
        choose,
        mesh=mesh,
        in_specs=(P(None, "basis"), P("basis", "band"), P("band"), P(), P()),
        out_specs=(P(), P()),
        check_vma=False,
    )
```

```python
import functools

import jax
import jax.numpy as jnp
from jax import lax
from jax.experimental import pallas as pl
from jax.experimental.pallas import tpu as pltpu
from jax.sharding import PartitionSpec as P

LANES = 128
VMEM_LIMIT = 55 * 2**20


def weighted_pairs(coeffs, band_weights):
    scaled = coeffs * band_weights[None, :]
    return lax.dot_general(
        scaled,
        coeffs,
        (((1,), (1,)), ((), ())),
        precision=lax.Precision.HIGHEST,
        preferred_element_type=jnp.float32,
    )


def gaunt_density(density_matrix, gaunt_index, gaunt_value):
    harmonics = density_matrix.shape[0] // 2
    codes = jnp.arange(harmonics, dtype=jnp.int32)[:, None]
    first_table = (gaunt_index[0][None, :] == codes).astype(jnp.float32)
    second_table = (gaunt_index[1][None, :] == codes).astype(jnp.float32)
    target_table = (gaunt_index[2][None, :] == codes).astype(jnp.float32)
    collected = []
    for radial in range(2):
        for other in range(2):
            block = density_matrix[
                radial * harmonics : (radial + 1) * harmonics,
                other * harmonics : (other + 1) * harmonics,
            ]
            spread = jnp.dot(
                block,
                second_table,
                precision=lax.Precision.HIGHEST,
                preferred_element_type=jnp.float32,
            )
            picked = jnp.sum(spread * first_table, axis=0)
            collected.append(picked * gaunt_value)
    values = jnp.stack(collected)
    return lax.dot_general(
        values,
        target_table,
        (((1,), (1,)), ((), ())),
        precision=lax.Precision.HIGHEST,
        preferred_element_type=jnp.float32,
    )


def split_columns(ref, part, columns):
    return ref.at[:, pl.ds(pl.multiple_of(part * columns, 128), columns)]


def leaving_kernel(columns, part_ref, matching_hbm, vectors_hbm, out_ref, matching, ahead, vectors, sems):
    depth = vectors.shape[0]
    middle = depth // 2
    mine = split_columns(vectors_hbm, part_ref[0], columns)
    other = split_columns(vectors_hbm, 1 - part_ref[0], columns)
    first = pltpu.make_async_copy(matching_hbm, matching, sems.at[0])
    upper = pltpu.make_async_copy(mine.at[:middle], vectors.at[:middle], sems.at[1])
    lower = pltpu.make_async_copy(mine.at[middle:], vectors.at[middle:], sems.at[2])
    later = pltpu.make_async_copy(other.at[:middle], ahead, sems.at[3])
    first.start()
    upper.start()
    lower.start()
    later.start()
    first.wait()
    upper.wait()
    out_ref[...] = jnp.dot(matching[:, :middle], vectors[:middle], preferred_element_type=jnp.float32)
    lower.wait()
    out_ref[...] += jnp.dot(matching[:, middle:], vectors[middle:], preferred_element_type=jnp.float32)
    later.wait()


def staying_kernel(columns, part_ref, matching, ahead, vectors_hbm, out_ref, vectors, sem):
    middle = ahead.shape[0]
    mine = split_columns(vectors_hbm, part_ref[0], columns)
    lower = pltpu.make_async_copy(mine.at[middle:], vectors, sem)
    lower.start()
    out_ref[...] = jnp.dot(matching[:, :middle], ahead[...], preferred_element_type=jnp.float32)
    lower.wait()
    out_ref[...] += jnp.dot(matching[:, middle:], vectors[...], preferred_element_type=jnp.float32)


VMEM = pl.BlockSpec(memory_space=pltpu.VMEM)
SMEM = pl.BlockSpec(memory_space=pltpu.SMEM)
HBM = pl.BlockSpec(memory_space=pltpu.HBM)


def cost(channels, depth, columns):
    return pl.CostEstimate(
        flops=2 * channels * depth * columns,
        bytes_accessed=2 * depth * (columns + channels) + 4 * channels * columns,
        transcendentals=0,
    )


def leaving_product(matching, vectors, part, columns):
    channels, depth = matching.shape
    return pl.pallas_call(
        functools.partial(leaving_kernel, columns),
        out_shape=(
            jax.ShapeDtypeStruct((channels, columns), jnp.float32),
            jax.ShapeDtypeStruct(matching.shape, matching.dtype),
            jax.ShapeDtypeStruct((depth // 2, columns), vectors.dtype),
        ),
        in_specs=[SMEM, HBM, HBM],
        out_specs=(VMEM, VMEM, VMEM),
        scratch_shapes=[
            pltpu.VMEM((depth, columns), vectors.dtype),
            pltpu.SemaphoreType.DMA((4,)),
        ],
        compiler_params=pltpu.CompilerParams(vmem_limit_bytes=VMEM_LIMIT),
        cost_estimate=cost(channels, depth, columns),
        name="leaving_product",
    )(part.reshape(1), matching, vectors)


def staying_product(matching, ahead, vectors, part, columns):
    channels, depth = matching.shape
    return pl.pallas_call(
        functools.partial(staying_kernel, columns),
        out_shape=jax.ShapeDtypeStruct((channels, columns), jnp.float32),
        in_specs=[SMEM, VMEM, VMEM, HBM],
        out_specs=VMEM,
        scratch_shapes=[
            pltpu.VMEM((depth - depth // 2, columns), vectors.dtype),
            pltpu.SemaphoreType.DMA,
        ],
        compiler_params=pltpu.CompilerParams(vmem_limit_bytes=VMEM_LIMIT),
        cost_estimate=cost(channels, depth, columns),
        name="staying_product",
    )(part.reshape(1), matching, ahead, vectors)


def tables_kernel(harmonics, index_ref, value_ref, second_ref, first_ref, target_ref):
    entries = index_ref.shape[1]
    wide = second_ref.shape[0]
    rows = lax.broadcasted_iota(jnp.int32, (wide, entries), 0)
    spot = index_ref[1:2, :]
    hit = (rows == spot) | (rows == spot + harmonics) | (rows == spot + 2 * harmonics)
    second_ref[...] = jnp.where(hit, 1.0, 0.0).astype(jnp.bfloat16)
    rows = lax.broadcasted_iota(jnp.int32, (first_ref.shape[0], entries), 0)
    first_ref[...] = jnp.where(rows == index_ref[0:1, :], value_ref[...], 0.0)
    rows = lax.broadcasted_iota(jnp.int32, (target_ref.shape[0], entries), 0)
    target_ref[...] = jnp.where(rows == index_ref[2:3, :], 1.0, 0.0).astype(jnp.bfloat16)


def round_up(value, unit):
    return -(-value // unit) * unit


def gaunt_tables(gaunt_index, gaunt_value, harmonics):
    entries = gaunt_value.shape[0]
    rows = round_up(harmonics, 8)
    wide = round_up(3 * harmonics, 128)
    shapes = (
        jax.ShapeDtypeStruct((wide, entries), jnp.bfloat16),
        jax.ShapeDtypeStruct((rows, entries), jnp.float32),
        jax.ShapeDtypeStruct((round_up(harmonics, 128), entries), jnp.bfloat16),
    )
    return pl.pallas_call(
        functools.partial(tables_kernel, harmonics),
        out_shape=shapes,
        in_specs=[VMEM, VMEM],
        out_specs=(VMEM, VMEM, VMEM),
        compiler_params=pltpu.CompilerParams(vmem_limit_bytes=32 * 2**20),
        cost_estimate=pl.CostEstimate(flops=8 * 2**20, bytes_accessed=5 * 2**20, transcendentals=0),
        name="gaunt_tables",
    )(gaunt_index, gaunt_value.reshape(1, entries))


def thirds(value):
    high = value.astype(jnp.bfloat16)
    rest = value - high.astype(jnp.float32)
    middle = rest.astype(jnp.bfloat16)
    return high, middle, (rest - middle.astype(jnp.float32)).astype(jnp.bfloat16)


def finish_kernel(tile, top_ref, bottom_ref, second_ref, first_ref, target_ref, matrix_ref, density_ref, left, values):
    channels = matrix_ref.shape[0]
    harmonics = channels // 2
    extra = channels - LANES
    half = top_ref.shape[0]
    upper = jnp.concatenate([top_ref[...], bottom_ref[: LANES - half, :]], axis=0)
    lower = bottom_ref[LANES - half : LANES - half + extra, :]
    rows = lax.broadcasted_iota(jnp.int32, (LANES, LANES), 0)
    lanes = lax.broadcasted_iota(jnp.int32, (LANES, LANES), 1)
    corner_there = (rows < extra) & (lanes >= LANES // 2) & (lanes < LANES // 2 + extra)
    main = jnp.where(corner_there, jnp.transpose(upper), upper)
    corner = pltpu.roll(upper, LANES // 2, 1)
    matrix_ref[:LANES, :LANES] = main
    matrix_ref[LANES:, :LANES] = lower
    side = bottom_ref.shape[0] - (LANES - half)
    tall = jnp.concatenate(
        [bottom_ref[LANES - half :, :], jnp.zeros((LANES - side, LANES), jnp.float32)], axis=0
    )
    matrix_ref[:LANES, LANES:] = jnp.transpose(tall)[:, :extra]
    matrix_ref[LANES:, LANES:] = corner[:extra, :extra]

    rows_in = first_ref.shape[0]
    left[...] = jnp.zeros_like(left)
    for radial in range(2):
        for other in range(2):
            block = matrix_ref[
                radial * harmonics : (radial + 1) * harmonics, other * harmonics : (other + 1) * harmonics
            ]
            at = (2 * radial + other) * rows_in
            for part, piece in enumerate(thirds(block)):
                left[at : at + harmonics, part * harmonics : (part + 1) * harmonics] = piece.astype(jnp.float32)
    stacked = left[...].astype(jnp.bfloat16)
    values[...] = jnp.zeros_like(values)
    entries = second_ref.shape[1]
    for start in range(0, entries, tile):
        columns = slice(start, start + tile)
        spread = jnp.dot(stacked, second_ref[:, columns], preferred_element_type=jnp.float32)
        for pair in range(4):
            chosen = spread[pair * rows_in : (pair + 1) * rows_in, :] * first_ref[:, columns]
            values[pair : pair + 1, columns] = jnp.sum(chosen, axis=0, keepdims=True)
    total = jnp.zeros((8, target_ref.shape[0]), jnp.float32)
    for piece in thirds(values[...]):
        total = total + lax.dot_general(
            piece, target_ref[...], (((1,), (1,)), ((), ())), preferred_element_type=jnp.float32
        )
    density_ref[...] = total[:4, :harmonics]


def finish(top, bottom, tables, channels):
    second, first, target = tables
    entries = second.shape[1]
    harmonics = channels // 2
    tile = 512 if entries % 512 == 0 else entries
    return pl.pallas_call(
        functools.partial(finish_kernel, tile),
        out_shape=(
            jax.ShapeDtypeStruct((channels, channels), jnp.float32),
            jax.ShapeDtypeStruct((4, harmonics), jnp.float32),
        ),
        in_specs=[VMEM] * 5,
        out_specs=(VMEM, VMEM),
        scratch_shapes=[
            pltpu.VMEM((4 * first.shape[0], second.shape[0]), jnp.float32),
            pltpu.VMEM((8, entries), jnp.float32),
        ],
        compiler_params=pltpu.CompilerParams(vmem_limit_bytes=32 * 2**20),
        name="finish",
    )(top, bottom, second, first, target)


def pack(matrix):
    channels = matrix.shape[0]
    extra = channels - LANES
    half = LANES // 2
    corner = jnp.pad(matrix[LANES:, LANES:], ((0, channels - extra), (half, LANES - half - extra)))
    rows = lax.broadcasted_iota(jnp.int32, (channels, LANES), 0)
    lanes = lax.broadcasted_iota(jnp.int32, (channels, LANES), 1)
    there = (rows < extra) & (lanes >= half) & (lanes < half + extra)
    packed = jnp.where(there, corner, matrix[:, :LANES])
    height = round_up(channels, 16) // 2
    height = round_up(height, 8)
    return packed[:height], jnp.pad(packed[height:], ((0, 2 * height - channels), (0, 0)))


def plain_body(matching, vectors, weights, gaunt_index, gaunt_value):
    partial_value = jnp.dot(matching, vectors, preferred_element_type=jnp.float32)
    summed = lax.psum(partial_value, "basis")
    local_terms = weighted_pairs(summed, weights)
    density_matrix = lax.psum(local_terms, "band")
    return (density_matrix, gaunt_density(density_matrix, gaunt_index, gaunt_value))


def halves(block, bit):
    middle = block.shape[1] // 2
    low, high = block[:, :middle], block[:, middle:]
    return jnp.where(bit == 1, low, high), jnp.where(bit == 1, high, low)


def body(basis, band, matching, vectors, weights, gaunt_index, gaunt_value):
    index = lax.axis_index("basis")
    levels = basis.bit_length() - 1
    channels, columns = matching.shape[0], vectors.shape[1]
    bits = [(index >> level) & 1 for level in range(levels)]
    own = functools.reduce(jnp.bitwise_xor, bits)

    def exchange(block, mask, band_mask=0):
        pairs = [
            (i * band + j, (i ^ mask) * band + (j ^ band_mask))
            for i in range(basis)
            for j in range(band)
        ]
        return lax.ppermute(block, ("basis", "band"), pairs)

    leaving, matching, ahead = leaving_product(matching, vectors, 1 - own, columns // 2)
    arriving = exchange(leaving, 1)
    staying = staying_product(matching, ahead, vectors, own, columns // 2)
    total = staying + arriving
    width = columns // 4
    sent_a, kept_a = halves(total[:, :width], bits[1])
    sent_b, kept_b = halves(total[:, width:], bits[2])
    come_a, come_b = exchange(sent_a, 3), exchange(sent_b, 5)
    sent_a, kept_a = halves(kept_a + come_a, bits[2])
    sent_b, kept_b = halves(kept_b + come_b, bits[1])
    come_a, come_b = exchange(sent_a, 5), exchange(sent_b, 3)
    block = jnp.concatenate([kept_a + come_a, kept_b + come_b], axis=1)
    width = columns // 16
    begin = own * (columns // 2)
    block_weights = jnp.concatenate(
        [
            lax.dynamic_slice_in_dim(weights, begin + (2 * bits[1] + bits[2]) * width, width),
            lax.dynamic_slice_in_dim(weights, begin + columns // 4 + (2 * bits[2] + bits[1]) * width, width),
        ]
    )
    for level in range(3, levels - 1):
        sent, kept = halves(block, bits[level])
        block = kept + exchange(sent, 1 | (1 << level))
        middle = block_weights.shape[0] // 2
        block_weights = jnp.where(bits[level] == 1, block_weights[middle:], block_weights[:middle])
    tied = lax.optimization_barrier((block, gaunt_index, gaunt_value))
    tables = gaunt_tables(tied[1], tied[2], channels // 2)
    block = block + exchange(tied[0], 1 | (1 << (levels - 1)))

    top, bottom = pack(weighted_pairs(block, block_weights))
    which = own
    for level in range(band.bit_length() - 1):
        which = which ^ ((lax.axis_index("band") >> level) & 1)
    sent = jnp.where(which == 1, top, bottom)
    terms = jnp.where(which == 1, bottom, top) + exchange(sent, 1)
    step = 1
    while step < band:
        terms = terms + exchange(terms, 1, step)
        step *= 2
    for level in range(1, levels - 1):
        terms = terms + exchange(terms, 1 | (1 << level))
    other = exchange(terms, 1)
    top = jnp.where(which == 1, other, terms)
    bottom = jnp.where(which == 1, terms, other)
    return finish(top, bottom, tables, channels)


def solution(mesh):
    basis, band = mesh.shape["basis"], mesh.shape["band"]

    def choose(*arrays):
        channels, depth = arrays[0].shape
        columns = arrays[1].shape[1]
        powers = basis & (basis - 1) == 0 and band & (band - 1) == 0 and basis >= 16
        sizes = columns % (16 * LANES) == 0 and depth % 256 == 0
        if powers and sizes and channels % 2 == 0 and LANES < channels <= LANES + LANES // 2:
            return body(basis, band, *arrays)
        return plain_body(*arrays)

    return jax.shard_map(
        choose,
        mesh=mesh,
        in_specs=(P(None, "basis"), P("basis", "band"), P("band"), P(), P()),
        out_specs=(P(), P()),
        check_vma=False,
    )
```

```python
import functools

import jax
import jax.numpy as jnp
from jax import lax
from jax.experimental import pallas as pl
from jax.experimental.pallas import tpu as pltpu
from jax.sharding import PartitionSpec as P

LANES = 128
VMEM_LIMIT = 52 * 2**20


def weighted_pairs(coeffs, band_weights):
    scaled = coeffs * band_weights[None, :]
    return lax.dot_general(
        scaled,
        coeffs,
        (((1,), (1,)), ((), ())),
        precision=lax.Precision.HIGHEST,
        preferred_element_type=jnp.float32,
    )


def gaunt_density(density_matrix, gaunt_index, gaunt_value):
    harmonics = density_matrix.shape[0] // 2
    codes = jnp.arange(harmonics, dtype=jnp.int32)[:, None]
    first_table = (gaunt_index[0][None, :] == codes).astype(jnp.float32)
    second_table = (gaunt_index[1][None, :] == codes).astype(jnp.float32)
    target_table = (gaunt_index[2][None, :] == codes).astype(jnp.float32)
    collected = []
    for radial in range(2):
        for other in range(2):
            block = density_matrix[
                radial * harmonics : (radial + 1) * harmonics,
                other * harmonics : (other + 1) * harmonics,
            ]
            spread = jnp.dot(
                block,
                second_table,
                precision=lax.Precision.HIGHEST,
                preferred_element_type=jnp.float32,
            )
            picked = jnp.sum(spread * first_table, axis=0)
            collected.append(picked * gaunt_value)
    values = jnp.stack(collected)
    return lax.dot_general(
        values,
        target_table,
        (((1,), (1,)), ((), ())),
        precision=lax.Precision.HIGHEST,
        preferred_element_type=jnp.float32,
    )


def split_columns(ref, part, columns):
    return ref.at[:, pl.ds(pl.multiple_of(part * columns, 128), columns)]


def leaving_kernel(columns, part_ref, matching_hbm, vectors_hbm, out_ref, matching, ahead, vectors, sems):
    depth = vectors.shape[0]
    middle = depth // 2
    mine = split_columns(vectors_hbm, part_ref[0], columns)
    other = split_columns(vectors_hbm, 1 - part_ref[0], columns)
    first = pltpu.make_async_copy(matching_hbm, matching, sems.at[0])
    upper = pltpu.make_async_copy(mine.at[:middle], vectors.at[:middle], sems.at[1])
    lower = pltpu.make_async_copy(mine.at[middle:], vectors.at[middle:], sems.at[2])
    later = pltpu.make_async_copy(other.at[: ahead.shape[0]], ahead, sems.at[3])
    first.start()
    upper.start()
    lower.start()
    later.start()
    first.wait()
    upper.wait()
    out_ref[...] = jnp.dot(matching[:, :middle], vectors[:middle], preferred_element_type=jnp.float32)
    lower.wait()
    out_ref[...] += jnp.dot(matching[:, middle:], vectors[middle:], preferred_element_type=jnp.float32)
    later.wait()


def staying_kernel(columns, part_ref, matching, ahead, vectors_hbm, out_ref, vectors, sem):
    middle = ahead.shape[0]
    mine = split_columns(vectors_hbm, part_ref[0], columns)
    lower = pltpu.make_async_copy(mine.at[middle:], vectors, sem)
    lower.start()
    out_ref[...] = jnp.dot(matching[:, :middle], ahead[...], preferred_element_type=jnp.float32)
    lower.wait()
    out_ref[...] += jnp.dot(matching[:, middle:], vectors[...], preferred_element_type=jnp.float32)


VMEM = pl.BlockSpec(memory_space=pltpu.VMEM)
SMEM = pl.BlockSpec(memory_space=pltpu.SMEM)
HBM = pl.BlockSpec(memory_space=pltpu.HBM)


def rows_ahead(depth):
    return depth * 2 // 5 // LANES * LANES


def cost(channels, depth, columns):
    return pl.CostEstimate(
        flops=2 * channels * depth * columns,
        bytes_accessed=2 * depth * (columns + channels) + 4 * channels * columns,
        transcendentals=0,
    )


def leaving_product(matching, vectors, part, columns):
    channels, depth = matching.shape
    return pl.pallas_call(
        functools.partial(leaving_kernel, columns),
        out_shape=(
            jax.ShapeDtypeStruct((channels, columns), jnp.float32),
            jax.ShapeDtypeStruct(matching.shape, matching.dtype),
            jax.ShapeDtypeStruct((rows_ahead(depth), columns), vectors.dtype),
        ),
        in_specs=[SMEM, HBM, HBM],
        out_specs=(VMEM, VMEM, VMEM),
        scratch_shapes=[
            pltpu.VMEM((depth, columns), vectors.dtype),
            pltpu.SemaphoreType.DMA((4,)),
        ],
        compiler_params=pltpu.CompilerParams(vmem_limit_bytes=VMEM_LIMIT),
        cost_estimate=cost(channels, depth, columns),
        name="leaving_product",
    )(part.reshape(1), matching, vectors)


def staying_product(matching, ahead, vectors, part, columns):
    channels, depth = matching.shape
    return pl.pallas_call(
        functools.partial(staying_kernel, columns),
        out_shape=jax.ShapeDtypeStruct((channels, columns), jnp.float32),
        in_specs=[SMEM, VMEM, VMEM, HBM],
        out_specs=VMEM,
        scratch_shapes=[
            pltpu.VMEM((depth - rows_ahead(depth), columns), vectors.dtype),
            pltpu.SemaphoreType.DMA,
        ],
        compiler_params=pltpu.CompilerParams(vmem_limit_bytes=VMEM_LIMIT),
        cost_estimate=cost(channels, depth, columns),
        name="staying_product",
    )(part.reshape(1), matching, ahead, vectors)


def tables_kernel(harmonics, index_ref, value_ref, second_ref, first_ref, target_ref):
    entries = index_ref.shape[1]
    wide = second_ref.shape[0]
    rows = lax.broadcasted_iota(jnp.int32, (wide, entries), 0)
    spot = index_ref[1:2, :]
    hit = (rows == spot) | (rows == spot + harmonics) | (rows == spot + 2 * harmonics)
    second_ref[...] = jnp.where(hit, 1.0, 0.0).astype(jnp.bfloat16)
    rows = lax.broadcasted_iota(jnp.int32, (first_ref.shape[0], entries), 0)
    first_ref[...] = jnp.where(rows == index_ref[0:1, :], value_ref[...], 0.0)
    rows = lax.broadcasted_iota(jnp.int32, (target_ref.shape[0], entries), 0)
    target_ref[...] = jnp.where(rows == index_ref[2:3, :], 1.0, 0.0).astype(jnp.bfloat16)


def round_up(value, unit):
    return -(-value // unit) * unit


def gaunt_tables(gaunt_index, gaunt_value, harmonics):
    entries = gaunt_value.shape[0]
    rows = round_up(harmonics, 8)
    wide = round_up(3 * harmonics, 128)
    shapes = (
        jax.ShapeDtypeStruct((wide, entries), jnp.bfloat16),
        jax.ShapeDtypeStruct((rows, entries), jnp.float32),
        jax.ShapeDtypeStruct((round_up(harmonics, 128), entries), jnp.bfloat16),
    )
    return pl.pallas_call(
        functools.partial(tables_kernel, harmonics),
        out_shape=shapes,
        in_specs=[VMEM, VMEM],
        out_specs=(VMEM, VMEM, VMEM),
        compiler_params=pltpu.CompilerParams(vmem_limit_bytes=32 * 2**20),
        cost_estimate=pl.CostEstimate(flops=8 * 2**20, bytes_accessed=5 * 2**20, transcendentals=0),
        name="gaunt_tables",
    )(gaunt_index, gaunt_value.reshape(1, entries))


def thirds(value):
    high = value.astype(jnp.bfloat16)
    rest = value - high.astype(jnp.float32)
    middle = rest.astype(jnp.bfloat16)
    return high, middle, (rest - middle.astype(jnp.float32)).astype(jnp.bfloat16)


def finish_kernel(tile, top_ref, bottom_ref, second_ref, first_ref, target_ref, matrix_ref, density_ref, left, values):
    channels = matrix_ref.shape[0]
    harmonics = channels // 2
    extra = channels - LANES
    half = top_ref.shape[0]
    upper = jnp.concatenate([top_ref[...], bottom_ref[: LANES - half, :]], axis=0)
    lower = bottom_ref[LANES - half : LANES - half + extra, :]
    rows = lax.broadcasted_iota(jnp.int32, (LANES, LANES), 0)
    lanes = lax.broadcasted_iota(jnp.int32, (LANES, LANES), 1)
    corner_there = (rows < extra) & (lanes >= LANES // 2) & (lanes < LANES // 2 + extra)
    main = jnp.where(corner_there, jnp.transpose(upper), upper)
    corner = pltpu.roll(upper, LANES // 2, 1)
    matrix_ref[:LANES, :LANES] = main
    matrix_ref[LANES:, :LANES] = lower
    side = bottom_ref.shape[0] - (LANES - half)
    tall = jnp.concatenate(
        [bottom_ref[LANES - half :, :], jnp.zeros((LANES - side, LANES), jnp.float32)], axis=0
    )
    matrix_ref[:LANES, LANES:] = jnp.transpose(tall)[:, :extra]
    matrix_ref[LANES:, LANES:] = corner[:extra, :extra]

    rows_in = first_ref.shape[0]
    left[...] = jnp.zeros_like(left)
    for radial in range(2):
        for other in range(2):
            block = matrix_ref[
                radial * harmonics : (radial + 1) * harmonics, other * harmonics : (other + 1) * harmonics
            ]
            at = (2 * radial + other) * rows_in
            for part, piece in enumerate(thirds(block)):
                left[at : at + harmonics, part * harmonics : (part + 1) * harmonics] = piece.astype(jnp.float32)
    stacked = left[...].astype(jnp.bfloat16)
    values[...] = jnp.zeros_like(values)
    entries = second_ref.shape[1]
    for start in range(0, entries, tile):
        columns = slice(start, start + tile)
        spread = jnp.dot(stacked, second_ref[:, columns], preferred_element_type=jnp.float32)
        for pair in range(4):
            chosen = spread[pair * rows_in : (pair + 1) * rows_in, :] * first_ref[:, columns]
            values[pair : pair + 1, columns] = jnp.sum(chosen, axis=0, keepdims=True)
    total = jnp.zeros((8, target_ref.shape[0]), jnp.float32)
    for piece in thirds(values[...]):
        total = total + lax.dot_general(
            piece, target_ref[...], (((1,), (1,)), ((), ())), preferred_element_type=jnp.float32
        )
    density_ref[...] = total[:4, :harmonics]


def finish(top, bottom, tables, channels):
    second, first, target = tables
    entries = second.shape[1]
    harmonics = channels // 2
    tile = 512 if entries % 512 == 0 else entries
    return pl.pallas_call(
        functools.partial(finish_kernel, tile),
        out_shape=(
            jax.ShapeDtypeStruct((channels, channels), jnp.float32),
            jax.ShapeDtypeStruct((4, harmonics), jnp.float32),
        ),
        in_specs=[VMEM] * 5,
        out_specs=(VMEM, VMEM),
        scratch_shapes=[
            pltpu.VMEM((4 * first.shape[0], second.shape[0]), jnp.float32),
            pltpu.VMEM((8, entries), jnp.float32),
        ],
        compiler_params=pltpu.CompilerParams(vmem_limit_bytes=32 * 2**20),
        name="finish",
    )(top, bottom, second, first, target)


def pack(matrix):
    channels = matrix.shape[0]
    extra = channels - LANES
    half = LANES // 2
    corner = jnp.pad(matrix[LANES:, LANES:], ((0, channels - extra), (half, LANES - half - extra)))
    rows = lax.broadcasted_iota(jnp.int32, (channels, LANES), 0)
    lanes = lax.broadcasted_iota(jnp.int32, (channels, LANES), 1)
    there = (rows < extra) & (lanes >= half) & (lanes < half + extra)
    packed = jnp.where(there, corner, matrix[:, :LANES])
    height = round_up(channels, 16) // 2
    height = round_up(height, 8)
    return packed[:height], jnp.pad(packed[height:], ((0, 2 * height - channels), (0, 0)))


def plain_body(matching, vectors, weights, gaunt_index, gaunt_value):
    partial_value = jnp.dot(matching, vectors, preferred_element_type=jnp.float32)
    summed = lax.psum(partial_value, "basis")
    local_terms = weighted_pairs(summed, weights)
    density_matrix = lax.psum(local_terms, "band")
    return (density_matrix, gaunt_density(density_matrix, gaunt_index, gaunt_value))


def halves(block, bit):
    middle = block.shape[1] // 2
    low, high = block[:, :middle], block[:, middle:]
    return jnp.where(bit == 1, low, high), jnp.where(bit == 1, high, low)


def body(basis, band, matching, vectors, weights, gaunt_index, gaunt_value):
    index = lax.axis_index("basis")
    levels = basis.bit_length() - 1
    channels, columns = matching.shape[0], vectors.shape[1]
    bits = [(index >> level) & 1 for level in range(levels)]
    own = functools.reduce(jnp.bitwise_xor, bits)

    def exchange(block, mask, band_mask=0):
        pairs = [
            (i * band + j, (i ^ mask) * band + (j ^ band_mask))
            for i in range(basis)
            for j in range(band)
        ]
        return lax.ppermute(block, ("basis", "band"), pairs)

    leaving, matching, ahead = leaving_product(matching, vectors, 1 - own, columns // 2)
    arriving = exchange(leaving, 1)
    staying = staying_product(matching, ahead, vectors, own, columns // 2)
    total = staying + arriving
    width = columns // 4
    sent_a, kept_a = halves(total[:, :width], bits[1])
    sent_b, kept_b = halves(total[:, width:], bits[2])
    come_a, come_b = exchange(sent_a, 3), exchange(sent_b, 5)
    sent_a, kept_a = halves(kept_a + come_a, bits[2])
    sent_b, kept_b = halves(kept_b + come_b, bits[1])
    come_a, come_b = exchange(sent_a, 5), exchange(sent_b, 3)
    block = jnp.concatenate([kept_a + come_a, kept_b + come_b], axis=1)
    width = columns // 16
    begin = own * (columns // 2)
    block_weights = jnp.concatenate(
        [
            lax.dynamic_slice_in_dim(weights, begin + (2 * bits[1] + bits[2]) * width, width),
            lax.dynamic_slice_in_dim(weights, begin + columns // 4 + (2 * bits[2] + bits[1]) * width, width),
        ]
    )
    for level in range(3, levels - 1):
        sent, kept = halves(block, bits[level])
        block = kept + exchange(sent, 1 | (1 << level))
        middle = block_weights.shape[0] // 2
        block_weights = jnp.where(bits[level] == 1, block_weights[middle:], block_weights[:middle])
    tied = lax.optimization_barrier((block, gaunt_index, gaunt_value))
    tables = gaunt_tables(tied[1], tied[2], channels // 2)
    come = exchange(tied[0], 1 | (1 << (levels - 1)))
    come, tables = lax.optimization_barrier((come, tables))
    block = block + come

    top, bottom = pack(weighted_pairs(block, block_weights))
    which = own
    for level in range(band.bit_length() - 1):
        which = which ^ ((lax.axis_index("band") >> level) & 1)
    sent = jnp.where(which == 1, top, bottom)
    terms = jnp.where(which == 1, bottom, top) + exchange(sent, 1)
    step = 1
    while step < band:
        terms = terms + exchange(terms, 1, step)
        step *= 2
    for level in range(1, levels - 1):
        terms = terms + exchange(terms, 1 | (1 << level))
    other = exchange(terms, 1)
    top = jnp.where(which == 1, other, terms)
    bottom = jnp.where(which == 1, terms, other)
    return finish(top, bottom, tables, channels)


def solution(mesh):
    basis, band = mesh.shape["basis"], mesh.shape["band"]

    def choose(*arrays):
        channels, depth = arrays[0].shape
        columns = arrays[1].shape[1]
        powers = basis & (basis - 1) == 0 and band & (band - 1) == 0 and basis >= 16
        sizes = columns % (16 * LANES) == 0 and depth % 256 == 0
        if powers and sizes and channels % 2 == 0 and LANES < channels <= LANES + LANES // 2:
            return body(basis, band, *arrays)
        return plain_body(*arrays)

    return jax.shard_map(
        choose,
        mesh=mesh,
        in_specs=(P(None, "basis"), P("basis", "band"), P("band"), P(), P()),
        out_specs=(P(), P()),
        check_vma=False,
    )
```

```python
import functools

import jax
import jax.numpy as jnp
from jax import lax
from jax.experimental import pallas as pl
from jax.experimental.pallas import tpu as pltpu
from jax.sharding import PartitionSpec as P

LANES = 128
TILE = 1024
LEAVING_STEPS, STAYING_STEPS, LAST_STEPS = 2, 1, 2
VMEM_LIMIT = 52 * 2**20


def weighted_pairs(coeffs, band_weights):
    scaled = coeffs * band_weights[None, :]
    return lax.dot_general(
        scaled,
        coeffs,
        (((1,), (1,)), ((), ())),
        precision=lax.Precision.HIGHEST,
        preferred_element_type=jnp.float32,
    )


def gaunt_density(density_matrix, gaunt_index, gaunt_value):
    harmonics = density_matrix.shape[0] // 2
    codes = jnp.arange(harmonics, dtype=jnp.int32)[:, None]
    first_table = (gaunt_index[0][None, :] == codes).astype(jnp.float32)
    second_table = (gaunt_index[1][None, :] == codes).astype(jnp.float32)
    target_table = (gaunt_index[2][None, :] == codes).astype(jnp.float32)
    collected = []
    for radial in range(2):
        for other in range(2):
            block = density_matrix[
                radial * harmonics : (radial + 1) * harmonics,
                other * harmonics : (other + 1) * harmonics,
            ]
            spread = jnp.dot(
                block,
                second_table,
                precision=lax.Precision.HIGHEST,
                preferred_element_type=jnp.float32,
            )
            picked = jnp.sum(spread * first_table, axis=0)
            collected.append(picked * gaunt_value)
    values = jnp.stack(collected)
    return lax.dot_general(
        values,
        target_table,
        (((1,), (1,)), ((), ())),
        precision=lax.Precision.HIGHEST,
        preferred_element_type=jnp.float32,
    )


def columns_of(ref, start, columns):
    return ref.at[:, pl.ds(pl.multiple_of(start, LANES), columns)]


def multiply(matching, pieces, out_ref):
    for at, (arrived, begin, end, vectors) in enumerate(pieces):
        arrived.wait()
        term = jnp.dot(matching[:, begin:end], vectors[begin:end, :], preferred_element_type=jnp.float32)
        if at == 0:
            out_ref[...] = term
        else:
            out_ref[...] += term


def fetch(source, target, sems, first, steps):
    depth = target.shape[0]
    pieces = []
    for step in range(steps):
        begin, end = depth * step // steps, depth * (step + 1) // steps
        copy = pltpu.make_async_copy(source.at[begin:end], target.at[begin:end], sems.at[first + step])
        copy.start()
        pieces.append((copy, begin, end, target))
    return pieces


def first_kernel(
    columns, own_ref, matching_hbm, vectors_hbm, leaving_ref, staying_ref, matching, vectors, vectors_a, sems
):
    own = own_ref[0]
    copy = pltpu.make_async_copy(matching_hbm, matching, sems.at[0])
    copy.start()
    leaving = fetch(columns_of(vectors_hbm, (1 - own) * columns, columns), vectors, sems, 1, LEAVING_STEPS)
    staying = fetch(
        columns_of(vectors_hbm, own * columns, columns // 2), vectors_a, sems, 1 + LEAVING_STEPS, STAYING_STEPS
    )
    copy.wait()
    multiply(matching, leaving, leaving_ref)
    multiply(matching, staying, staying_ref)


def second_kernel(columns, own_ref, matching, vectors_hbm, staying_ref, vectors, sems):
    start = own_ref[0] * columns + columns // 2
    multiply(matching, fetch(columns_of(vectors_hbm, start, columns // 2), vectors, sems, 0, LAST_STEPS), staying_ref)


VMEM = pl.BlockSpec(memory_space=pltpu.VMEM)
SMEM = pl.BlockSpec(memory_space=pltpu.SMEM)
HBM = pl.BlockSpec(memory_space=pltpu.HBM)


def cost(channels, depth, columns):
    return pl.CostEstimate(
        flops=2 * channels * depth * columns,
        bytes_accessed=2 * depth * (columns + channels) + 4 * channels * columns,
        transcendentals=0,
    )


def first_products(matching, vectors, own, columns):
    channels, depth = matching.shape
    return pl.pallas_call(
        functools.partial(first_kernel, columns),
        out_shape=(
            jax.ShapeDtypeStruct((channels, columns), jnp.float32),
            jax.ShapeDtypeStruct((channels, columns // 2), jnp.float32),
            jax.ShapeDtypeStruct(matching.shape, matching.dtype),
        ),
        in_specs=[SMEM, HBM, HBM],
        out_specs=(VMEM, VMEM, VMEM),
        scratch_shapes=[
            pltpu.VMEM((depth, columns), vectors.dtype),
            pltpu.VMEM((depth, columns // 2), vectors.dtype),
            pltpu.SemaphoreType.DMA((1 + LEAVING_STEPS + STAYING_STEPS,)),
        ],
        compiler_params=pltpu.CompilerParams(vmem_limit_bytes=VMEM_LIMIT),
        cost_estimate=cost(channels, depth, columns * 3 // 2),
        name="first_products",
    )(own.reshape(1), matching, vectors)


def second_products(matching, vectors, own, columns):
    channels, depth = matching.shape
    return pl.pallas_call(
        functools.partial(second_kernel, columns),
        out_shape=jax.ShapeDtypeStruct((channels, columns // 2), jnp.float32),
        in_specs=[SMEM, VMEM, HBM],
        out_specs=VMEM,
        scratch_shapes=[
            pltpu.VMEM((depth, columns // 2), vectors.dtype),
            pltpu.SemaphoreType.DMA((LAST_STEPS,)),
        ],
        compiler_params=pltpu.CompilerParams(vmem_limit_bytes=VMEM_LIMIT),
        cost_estimate=cost(channels, depth, columns // 2),
        name="second_products",
    )(own.reshape(1), matching, vectors)


def round_up(value, unit):
    return -(-value // unit) * unit


def tables_kernel(index_ref, value_ref, second_ref, first_ref, target_ref):
    entries = index_ref.shape[1]
    rows = lax.broadcasted_iota(jnp.int32, (LANES, entries), 0)
    hit = jnp.where(rows == index_ref[1:2, :], 1.0, 0.0).astype(jnp.bfloat16)
    second_ref[:LANES, :] = hit
    second_ref[LANES:, :] = hit
    first_rows = lax.broadcasted_iota(jnp.int32, (first_ref.shape[0], entries), 0)
    first_ref[...] = jnp.where(first_rows == index_ref[0:1, :], value_ref[...], 0.0)
    target_ref[...] = jnp.transpose(jnp.where(rows == index_ref[2:3, :], 1.0, 0.0)).astype(jnp.bfloat16)


def gaunt_tables(gaunt_index, gaunt_value, harmonics):
    entries = gaunt_value.shape[0]
    shapes = (
        jax.ShapeDtypeStruct((2 * LANES, entries), jnp.bfloat16),
        jax.ShapeDtypeStruct((round_up(harmonics, 8), entries), jnp.float32),
        jax.ShapeDtypeStruct((entries, LANES), jnp.bfloat16),
    )
    return pl.pallas_call(
        tables_kernel,
        out_shape=shapes,
        in_specs=[VMEM, VMEM],
        out_specs=(VMEM, VMEM, VMEM),
        compiler_params=pltpu.CompilerParams(vmem_limit_bytes=32 * 2**20),
        cost_estimate=pl.CostEstimate(flops=8 * 2**20, bytes_accessed=5 * 2**20, transcendentals=0),
        name="gaunt_tables",
    )(gaunt_index, gaunt_value.reshape(1, entries))


def two_parts(value):
    high = value.astype(jnp.bfloat16)
    return high, (value - high.astype(jnp.float32)).astype(jnp.bfloat16)


def finish_kernel(tile, top_ref, bottom_ref, second_ref, first_ref, target_ref, matrix_ref, density_ref, full):
    channels = matrix_ref.shape[0]
    harmonics = channels // 2
    extra = channels - LANES
    half = top_ref.shape[0]
    upper = jnp.concatenate([top_ref[...], bottom_ref[: LANES - half, :]], axis=0)
    rest = bottom_ref[LANES - half :, :]
    rows = lax.broadcasted_iota(jnp.int32, (LANES, LANES), 0)
    lanes = lax.broadcasted_iota(jnp.int32, (LANES, LANES), 1)
    corner_there = (rows < extra) & (lanes >= LANES // 2) & (lanes < LANES // 2 + extra)
    tall = jnp.concatenate([rest, jnp.zeros((LANES - rest.shape[0], LANES), jnp.float32)], axis=0)
    corner = pltpu.roll(upper, LANES // 2, 1)
    full[:LANES, :LANES] = jnp.where(corner_there, jnp.transpose(upper), upper)
    full[:LANES, LANES:] = jnp.transpose(tall)
    full[LANES:, :LANES] = jnp.zeros((full.shape[0] - LANES, LANES), jnp.float32)
    full[LANES : LANES + rest.shape[0], :LANES] = rest
    full[LANES:, LANES:] = jnp.zeros((full.shape[0] - LANES, LANES), jnp.float32)
    full[LANES:channels, LANES:] = corner[:extra]
    matrix_ref[...] = full[:channels, :channels]

    height = first_ref.shape[0]
    entries = second_ref.shape[1]
    blocks = []
    for radial in range(2):
        strip = full[radial * harmonics : radial * harmonics + height, :]
        blocks.append(strip[:, :LANES])
        blocks.append(pltpu.roll(strip, 2 * LANES - harmonics, 1)[:, :LANES])
    stacked = jnp.concatenate(two_parts(jnp.concatenate(blocks, axis=0)), axis=1)
    kept = []
    for start in range(0, entries, tile):
        columns = slice(start, start + tile)
        spread = jnp.dot(stacked, second_ref[:, columns], preferred_element_type=jnp.float32)
        picked = []
        for pair in range(4):
            partial_sum = jnp.zeros((8, tile), jnp.float32)
            for at in range(0, height, 8):
                here = spread[pair * height + at : pair * height + at + 8, :]
                partial_sum = partial_sum + here * first_ref[at : at + 8, columns]
            picked.append(partial_sum)
        kept.append(jnp.concatenate(two_parts(jnp.concatenate(picked, axis=0)), axis=0))
    total = jnp.dot(jnp.concatenate(kept, axis=1), target_ref[...], preferred_element_type=jnp.float32)
    for pair in range(4):
        both = total[8 * pair : 8 * pair + 8] + total[32 + 8 * pair : 40 + 8 * pair]
        density_ref[pair : pair + 1, :] = jnp.sum(both, axis=0, keepdims=True)[:, :harmonics]


def finish(top, bottom, tables, channels):
    second, first, target = tables
    entries = second.shape[1]
    harmonics = channels // 2
    tile = TILE if entries % TILE == 0 else entries
    return pl.pallas_call(
        functools.partial(finish_kernel, tile),
        out_shape=(
            jax.ShapeDtypeStruct((channels, channels), jnp.float32),
            jax.ShapeDtypeStruct((4, harmonics), jnp.float32),
        ),
        in_specs=[VMEM] * 5,
        out_specs=(VMEM, VMEM),
        scratch_shapes=[pltpu.VMEM((round_up(harmonics + first.shape[0], 16), 2 * LANES), jnp.float32)],
        compiler_params=pltpu.CompilerParams(vmem_limit_bytes=32 * 2**20),
        name="finish",
    )(top, bottom, second, first, target)


def pack(matrix):
    channels = matrix.shape[0]
    extra = channels - LANES
    half = LANES // 2
    corner = jnp.pad(matrix[LANES:, LANES:], ((0, channels - extra), (half, LANES - half - extra)))
    rows = lax.broadcasted_iota(jnp.int32, (channels, LANES), 0)
    lanes = lax.broadcasted_iota(jnp.int32, (channels, LANES), 1)
    there = (rows < extra) & (lanes >= half) & (lanes < half + extra)
    packed = jnp.where(there, corner, matrix[:, :LANES])
    height = round_up(channels, 16) // 2
    height = round_up(height, 8)
    return packed[:height], jnp.pad(packed[height:], ((0, 2 * height - channels), (0, 0)))


def plain_body(matching, vectors, weights, gaunt_index, gaunt_value):
    partial_value = jnp.dot(matching, vectors, preferred_element_type=jnp.float32)
    summed = lax.psum(partial_value, "basis")
    local_terms = weighted_pairs(summed, weights)
    density_matrix = lax.psum(local_terms, "band")
    return (density_matrix, gaunt_density(density_matrix, gaunt_index, gaunt_value))


def halves(block, bit):
    middle = block.shape[1] // 2
    low, high = block[:, :middle], block[:, middle:]
    return jnp.where(bit == 1, low, high), jnp.where(bit == 1, high, low)


def body(basis, band, matching, vectors, weights, gaunt_index, gaunt_value):
    index = lax.axis_index("basis")
    levels = basis.bit_length() - 1
    channels, columns = matching.shape[0], vectors.shape[1]
    bits = [(index >> level) & 1 for level in range(levels)]
    own = functools.reduce(jnp.bitwise_xor, bits)

    def exchange(block, mask, band_mask=0):
        pairs = [
            (i * band + j, (i ^ mask) * band + (j ^ band_mask))
            for i in range(basis)
            for j in range(band)
        ]
        return lax.ppermute(block, ("basis", "band"), pairs)

    leaving, staying_a, matching = first_products(matching, vectors, own, columns // 2)
    arriving = exchange(leaving, 1)
    staying_b = second_products(matching, vectors, own, columns // 2)
    width = columns // 4
    sent_a, kept_a = halves(staying_a + arriving[:, :width], bits[1])
    sent_b, kept_b = halves(staying_b + arriving[:, width:], bits[2])
    come_a, come_b = exchange(sent_a, 3), exchange(sent_b, 5)
    sent_a, kept_a = halves(kept_a + come_a, bits[2])
    sent_b, kept_b = halves(kept_b + come_b, bits[1])
    come_a, come_b = exchange(sent_a, 5), exchange(sent_b, 3)
    block = jnp.concatenate([kept_a + come_a, kept_b + come_b], axis=1)
    for level in range(3, levels - 1):
        sent, kept = halves(block, bits[level])
        block = kept + exchange(sent, 1 | (1 << level))
    block, weights, gaunt_index, gaunt_value = lax.optimization_barrier((block, weights, gaunt_index, gaunt_value))
    come = exchange(block, 1 | (1 << (levels - 1)))
    tables = gaunt_tables(gaunt_index, gaunt_value, channels // 2)
    width = columns // 16
    begin = own * (columns // 2)
    block_weights = jnp.concatenate(
        [
            lax.dynamic_slice_in_dim(weights, begin + (2 * bits[1] + bits[2]) * width, width),
            lax.dynamic_slice_in_dim(weights, begin + columns // 4 + (2 * bits[2] + bits[1]) * width, width),
        ]
    )
    for level in range(3, levels - 1):
        middle = block_weights.shape[0] // 2
        block_weights = jnp.where(bits[level] == 1, block_weights[middle:], block_weights[:middle])
    come, tables, block_weights = lax.optimization_barrier((come, tables, block_weights))
    block = block + come

    top, bottom = pack(weighted_pairs(block, block_weights))
    which = own
    for level in range(band.bit_length() - 1):
        which = which ^ ((lax.axis_index("band") >> level) & 1)
    sent = jnp.where(which == 1, top, bottom)
    terms = jnp.where(which == 1, bottom, top) + exchange(sent, 1)
    step = 1
    while step < band:
        terms = terms + exchange(terms, 1, step)
        step *= 2
    for level in range(1, levels - 1):
        terms = terms + exchange(terms, 1 | (1 << level))
    other = exchange(terms, 1)
    top = jnp.where(which == 1, other, terms)
    bottom = jnp.where(which == 1, terms, other)
    return finish(top, bottom, tables, channels)


def solution(mesh):
    basis, band = mesh.shape["basis"], mesh.shape["band"]

    def choose(*arrays):
        channels, depth = arrays[0].shape
        columns = arrays[1].shape[1]
        powers = basis & (basis - 1) == 0 and band & (band - 1) == 0 and basis >= 16
        sizes = columns % (16 * LANES) == 0 and depth % 256 == 0
        if powers and sizes and channels % 2 == 0 and LANES < channels <= LANES + LANES // 2:
            return body(basis, band, *arrays)
        return plain_body(*arrays)

    return jax.shard_map(
        choose,
        mesh=mesh,
        in_specs=(P(None, "basis"), P("basis", "band"), P("band"), P(), P()),
        out_specs=(P(), P()),
        check_vma=False,
    )
```

```python
import functools

import jax
import jax.numpy as jnp
from jax import lax
from jax.experimental import pallas as pl
from jax.experimental.pallas import tpu as pltpu
from jax.sharding import PartitionSpec as P

LANES = 128
TILE = 1024
LEAVING_STEPS, STAYING_STEPS, LAST_STEPS = 2, 1, 2
GROUP = 1
VMEM_LIMIT = 52 * 2**20


def weighted_pairs(coeffs, band_weights):
    scaled = coeffs * band_weights[None, :]
    return lax.dot_general(
        scaled,
        coeffs,
        (((1,), (1,)), ((), ())),
        precision=lax.Precision.HIGHEST,
        preferred_element_type=jnp.float32,
    )


def gaunt_density(density_matrix, gaunt_index, gaunt_value):
    harmonics = density_matrix.shape[0] // 2
    codes = jnp.arange(harmonics, dtype=jnp.int32)[:, None]
    first_table = (gaunt_index[0][None, :] == codes).astype(jnp.float32)
    second_table = (gaunt_index[1][None, :] == codes).astype(jnp.float32)
    target_table = (gaunt_index[2][None, :] == codes).astype(jnp.float32)
    collected = []
    for radial in range(2):
        for other in range(2):
            block = density_matrix[
                radial * harmonics : (radial + 1) * harmonics,
                other * harmonics : (other + 1) * harmonics,
            ]
            spread = jnp.dot(
                block,
                second_table,
                precision=lax.Precision.HIGHEST,
                preferred_element_type=jnp.float32,
            )
            picked = jnp.sum(spread * first_table, axis=0)
            collected.append(picked * gaunt_value)
    values = jnp.stack(collected)
    return lax.dot_general(
        values,
        target_table,
        (((1,), (1,)), ((), ())),
        precision=lax.Precision.HIGHEST,
        preferred_element_type=jnp.float32,
    )


def columns_of(ref, start, columns):
    return ref.at[:, pl.ds(pl.multiple_of(start, LANES), columns)]


def multiply(matching, pieces, out_ref):
    for at, (arrived, begin, end, vectors) in enumerate(pieces):
        arrived.wait()
        term = jnp.dot(matching[:, begin:end], vectors[begin:end, :], preferred_element_type=jnp.float32)
        if at == 0:
            out_ref[...] = term
        else:
            out_ref[...] += term


def fetch(source, target, sems, first, steps):
    depth = target.shape[0]
    pieces = []
    for step in range(steps):
        begin, end = depth * step // steps, depth * (step + 1) // steps
        copy = pltpu.make_async_copy(source.at[begin:end], target.at[begin:end], sems.at[first + step])
        copy.start()
        pieces.append((copy, begin, end, target))
    return pieces


def first_kernel(
    columns, own_ref, matching_hbm, vectors_hbm, leaving_ref, staying_ref, matching, vectors, vectors_a, sems
):
    own = own_ref[0]
    copy = pltpu.make_async_copy(matching_hbm, matching, sems.at[0])
    copy.start()
    leaving = fetch(columns_of(vectors_hbm, (1 - own) * columns, columns), vectors, sems, 1, LEAVING_STEPS)
    staying = fetch(
        columns_of(vectors_hbm, own * columns, columns // 2), vectors_a, sems, 1 + LEAVING_STEPS, STAYING_STEPS
    )
    copy.wait()
    multiply(matching, leaving, leaving_ref)
    multiply(matching, staying, staying_ref)


def second_kernel(columns, own_ref, matching, vectors_hbm, staying_ref, vectors, sems):
    start = own_ref[0] * columns + columns // 2
    multiply(matching, fetch(columns_of(vectors_hbm, start, columns // 2), vectors, sems, 0, LAST_STEPS), staying_ref)


VMEM = pl.BlockSpec(memory_space=pltpu.VMEM)
SMEM = pl.BlockSpec(memory_space=pltpu.SMEM)
HBM = pl.BlockSpec(memory_space=pltpu.HBM)


def cost(channels, depth, columns):
    return pl.CostEstimate(
        flops=2 * channels * depth * columns,
        bytes_accessed=2 * depth * (columns + channels) + 4 * channels * columns,
        transcendentals=0,
    )


def first_products(matching, vectors, own, columns):
    channels, depth = matching.shape
    return pl.pallas_call(
        functools.partial(first_kernel, columns),
        out_shape=(
            jax.ShapeDtypeStruct((channels, columns), jnp.float32),
            jax.ShapeDtypeStruct((channels, columns // 2), jnp.float32),
            jax.ShapeDtypeStruct(matching.shape, matching.dtype),
        ),
        in_specs=[SMEM, HBM, HBM],
        out_specs=(VMEM, VMEM, VMEM),
        scratch_shapes=[
            pltpu.VMEM((depth, columns), vectors.dtype),
            pltpu.VMEM((depth, columns // 2), vectors.dtype),
            pltpu.SemaphoreType.DMA((1 + LEAVING_STEPS + STAYING_STEPS,)),
        ],
        compiler_params=pltpu.CompilerParams(vmem_limit_bytes=VMEM_LIMIT),
        cost_estimate=cost(channels, depth, columns * 3 // 2),
        name="first_products",
    )(own.reshape(1), matching, vectors)


def second_products(matching, vectors, own, columns):
    channels, depth = matching.shape
    return pl.pallas_call(
        functools.partial(second_kernel, columns),
        out_shape=jax.ShapeDtypeStruct((channels, columns // 2), jnp.float32),
        in_specs=[SMEM, VMEM, HBM],
        out_specs=VMEM,
        scratch_shapes=[
            pltpu.VMEM((depth, columns // 2), vectors.dtype),
            pltpu.SemaphoreType.DMA((LAST_STEPS,)),
        ],
        compiler_params=pltpu.CompilerParams(vmem_limit_bytes=VMEM_LIMIT),
        cost_estimate=cost(channels, depth, columns // 2),
        name="second_products",
    )(own.reshape(1), matching, vectors)


def round_up(value, unit):
    return -(-value // unit) * unit


def tables_kernel(index_ref, value_ref, second_ref, first_ref, target_ref):
    entries = index_ref.shape[1]
    rows = lax.broadcasted_iota(jnp.int32, (LANES, entries), 0)
    hit = jnp.where(rows == index_ref[1:2, :], 1.0, 0.0).astype(jnp.bfloat16)
    second_ref[:LANES, :] = hit
    second_ref[LANES:, :] = hit
    first_rows = lax.broadcasted_iota(jnp.int32, (first_ref.shape[0], entries), 0)
    first_ref[...] = jnp.where(first_rows == index_ref[0:1, :], value_ref[...], 0.0)
    target_ref[...] = jnp.transpose(jnp.where(rows == index_ref[2:3, :], 1.0, 0.0)).astype(jnp.bfloat16)


def gaunt_tables(gaunt_index, gaunt_value, harmonics):
    entries = gaunt_value.shape[0]
    shapes = (
        jax.ShapeDtypeStruct((2 * LANES, entries), jnp.bfloat16),
        jax.ShapeDtypeStruct((round_up(harmonics, 8), entries), jnp.float32),
        jax.ShapeDtypeStruct((entries, LANES), jnp.bfloat16),
    )
    return pl.pallas_call(
        tables_kernel,
        out_shape=shapes,
        in_specs=[VMEM, VMEM],
        out_specs=(VMEM, VMEM, VMEM),
        compiler_params=pltpu.CompilerParams(vmem_limit_bytes=32 * 2**20),
        cost_estimate=pl.CostEstimate(flops=8 * 2**20, bytes_accessed=5 * 2**20, transcendentals=0),
        name="gaunt_tables",
    )(gaunt_index, gaunt_value.reshape(1, entries))


def two_parts(value):
    high = value.astype(jnp.bfloat16)
    return high, (value - high.astype(jnp.float32)).astype(jnp.bfloat16)


def finish_kernel(tile, top_ref, bottom_ref, second_ref, first_ref, target_ref, matrix_ref, density_ref, full):
    channels = matrix_ref.shape[0]
    harmonics = channels // 2
    extra = channels - LANES
    half = top_ref.shape[0]
    upper = jnp.concatenate([top_ref[...], bottom_ref[: LANES - half, :]], axis=0)
    rest = bottom_ref[LANES - half :, :]
    rows = lax.broadcasted_iota(jnp.int32, (LANES, LANES), 0)
    lanes = lax.broadcasted_iota(jnp.int32, (LANES, LANES), 1)
    corner_there = (rows < extra) & (lanes >= LANES // 2) & (lanes < LANES // 2 + extra)
    tall = jnp.concatenate([rest, jnp.zeros((LANES - rest.shape[0], LANES), jnp.float32)], axis=0)
    corner = pltpu.roll(upper, LANES // 2, 1)
    full[:LANES, :LANES] = jnp.where(corner_there, jnp.transpose(upper), upper)
    full[:LANES, LANES:] = jnp.transpose(tall)
    full[LANES:, :LANES] = jnp.zeros((full.shape[0] - LANES, LANES), jnp.float32)
    full[LANES : LANES + rest.shape[0], :LANES] = rest
    full[LANES:, LANES:] = jnp.zeros((full.shape[0] - LANES, LANES), jnp.float32)
    full[LANES:channels, LANES:] = corner[:extra]
    matrix_ref[...] = full[:channels, :channels]

    height = first_ref.shape[0]
    entries = second_ref.shape[1]
    blocks = []
    for radial in range(2):
        strip = full[radial * harmonics : radial * harmonics + height, :]
        blocks.append(strip[:, :LANES])
        blocks.append(pltpu.roll(strip, 2 * LANES - harmonics, 1)[:, :LANES])
    stacked = jnp.concatenate(two_parts(jnp.concatenate(blocks, axis=0)), axis=1)
    kept = []
    for start in range(0, entries, tile):
        columns = slice(start, start + tile)
        spread = jnp.dot(stacked, second_ref[:, columns], preferred_element_type=jnp.float32)
        picked = []
        for pair in range(4):
            partial_sum = jnp.zeros((8, tile), jnp.float32)
            for at in range(0, height, 8):
                here = spread[pair * height + at : pair * height + at + 8, :]
                partial_sum = partial_sum + here * first_ref[at : at + 8, columns]
            picked.append(partial_sum)
        kept.append(jnp.concatenate(two_parts(jnp.concatenate(picked, axis=0)), axis=0))
    total = jnp.dot(jnp.concatenate(kept, axis=1), target_ref[...], preferred_element_type=jnp.float32)
    for pair in range(4):
        both = total[8 * pair : 8 * pair + 8] + total[32 + 8 * pair : 40 + 8 * pair]
        density_ref[pair : pair + 1, :] = jnp.sum(both, axis=0, keepdims=True)[:, :harmonics]


def finish(top, bottom, tables, channels):
    second, first, target = tables
    entries = second.shape[1]
    harmonics = channels // 2
    tile = TILE if entries % TILE == 0 else entries
    return pl.pallas_call(
        functools.partial(finish_kernel, tile),
        out_shape=(
            jax.ShapeDtypeStruct((channels, channels), jnp.float32),
            jax.ShapeDtypeStruct((4, harmonics), jnp.float32),
        ),
        in_specs=[VMEM] * 5,
        out_specs=(VMEM, VMEM),
        scratch_shapes=[pltpu.VMEM((round_up(harmonics + first.shape[0], 16), 2 * LANES), jnp.float32)],
        compiler_params=pltpu.CompilerParams(vmem_limit_bytes=32 * 2**20),
        name="finish",
    )(top, bottom, second, first, target)


def pack(matrix):
    channels = matrix.shape[0]
    extra = channels - LANES
    half = LANES // 2
    corner = jnp.pad(matrix[LANES:, LANES:], ((0, channels - extra), (half, LANES - half - extra)))
    rows = lax.broadcasted_iota(jnp.int32, (channels, LANES), 0)
    lanes = lax.broadcasted_iota(jnp.int32, (channels, LANES), 1)
    there = (rows < extra) & (lanes >= half) & (lanes < half + extra)
    packed = jnp.where(there, corner, matrix[:, :LANES])
    height = round_up(channels, 16) // 2
    height = round_up(height, 8)
    return packed[:height], jnp.pad(packed[height:], ((0, 2 * height - channels), (0, 0)))


def plain_body(matching, vectors, weights, gaunt_index, gaunt_value):
    partial_value = jnp.dot(matching, vectors, preferred_element_type=jnp.float32)
    summed = lax.psum(partial_value, "basis")
    local_terms = weighted_pairs(summed, weights)
    density_matrix = lax.psum(local_terms, "band")
    return (density_matrix, gaunt_density(density_matrix, gaunt_index, gaunt_value))


def halves(block, bit):
    middle = block.shape[1] // 2
    low, high = block[:, :middle], block[:, middle:]
    return jnp.where(bit == 1, low, high), jnp.where(bit == 1, high, low)


def direct_sum(block, steps, exchange):
    arrived = [block]
    for which in range(1, 1 << len(steps)):
        mask = band_mask = 0
        for at, (on_basis, on_band) in enumerate(steps):
            if which >> at & 1:
                mask, band_mask = mask ^ on_basis, band_mask ^ on_band
        odd = (mask.bit_count() + band_mask.bit_count()) & 1
        arrived.append(exchange(block, mask | odd, band_mask))
    while len(arrived) > 1:
        arrived = [first + second for first, second in zip(arrived[::2], arrived[1::2])]
    return arrived[0]


def body(basis, band, matching, vectors, weights, gaunt_index, gaunt_value):
    index = lax.axis_index("basis")
    levels = basis.bit_length() - 1
    channels, columns = matching.shape[0], vectors.shape[1]
    bits = [(index >> level) & 1 for level in range(levels)]
    own = functools.reduce(jnp.bitwise_xor, bits)

    def exchange(block, mask, band_mask=0):
        pairs = [
            (i * band + j, (i ^ mask) * band + (j ^ band_mask))
            for i in range(basis)
            for j in range(band)
        ]
        return lax.ppermute(block, ("basis", "band"), pairs)

    leaving, staying_a, matching = first_products(matching, vectors, own, columns // 2)
    arriving = exchange(leaving, 1)
    staying_b = second_products(matching, vectors, own, columns // 2)
    width = columns // 8
    low, high = staying_a + arriving[:, : 2 * width], staying_b + arriving[:, 2 * width :]

    def quarter(first, second):
        pair = jnp.where(first == 1, high, low)
        return jnp.where(second == 1, pair[:, width:], pair[:, :width])

    come_b = exchange(quarter(1 - bits[1], 1 - bits[2]), 6)
    come_x = exchange(quarter(1 - bits[1], bits[2]), 3)
    come_z = exchange(quarter(bits[1], 1 - bits[2]), 5)
    block = quarter(bits[1], bits[2]) + come_x + come_z + come_b
    for level in range(3, levels - 1):
        sent, kept = halves(block, bits[level])
        block = kept + exchange(sent, 1 | (1 << level))
    block, weights, gaunt_index, gaunt_value = lax.optimization_barrier((block, weights, gaunt_index, gaunt_value))
    come = exchange(block, 1 | (1 << (levels - 1)))
    tables = gaunt_tables(gaunt_index, gaunt_value, channels // 2)
    begin = own * (columns // 2) + (2 * bits[1] + bits[2]) * width
    block_weights = lax.dynamic_slice_in_dim(weights, begin, width)
    for level in range(3, levels - 1):
        middle = block_weights.shape[0] // 2
        block_weights = jnp.where(bits[level] == 1, block_weights[middle:], block_weights[:middle])
    come, tables, block_weights = lax.optimization_barrier((come, tables, block_weights))
    block = block + come

    top, bottom = pack(weighted_pairs(block, block_weights))
    which = own
    for level in range(band.bit_length() - 1):
        which = which ^ ((lax.axis_index("band") >> level) & 1)
    sent = jnp.where(which == 1, top, bottom)
    terms = jnp.where(which == 1, bottom, top) + exchange(sent, 1)
    steps = [(0, 1 << level) for level in range(band.bit_length() - 1)]
    steps += [(1 << level, 0) for level in range(1, levels - 1)]
    for at in range(0, len(steps), GROUP):
        terms = direct_sum(terms, steps[at : at + GROUP], exchange)
    other = exchange(terms, 1)
    top = jnp.where(which == 1, other, terms)
    bottom = jnp.where(which == 1, terms, other)
    return finish(top, bottom, tables, channels)


def solution(mesh):
    basis, band = mesh.shape["basis"], mesh.shape["band"]

    def choose(*arrays):
        channels, depth = arrays[0].shape
        columns = arrays[1].shape[1]
        powers = basis & (basis - 1) == 0 and band & (band - 1) == 0 and basis >= 16
        sizes = columns % (16 * LANES) == 0 and depth % 256 == 0
        if powers and sizes and channels % 2 == 0 and LANES < channels <= LANES + LANES // 2:
            return body(basis, band, *arrays)
        return plain_body(*arrays)

    return jax.shard_map(
        choose,
        mesh=mesh,
        in_specs=(P(None, "basis"), P("basis", "band"), P("band"), P(), P()),
        out_specs=(P(), P()),
        check_vma=False,
    )
```

```python
import functools

import jax
import jax.numpy as jnp
from jax import lax
from jax.experimental import pallas as pl
from jax.experimental.pallas import tpu as pltpu
from jax.sharding import PartitionSpec as P

LANES = 128
TILE = 1024
LEAVING_STEPS, STAYING_STEPS, LAST_STEPS = 2, 1, 2
GROUP = 2
VMEM_LIMIT = 52 * 2**20


def weighted_pairs(coeffs, band_weights):
    scaled = coeffs * band_weights[None, :]
    return lax.dot_general(
        scaled,
        coeffs,
        (((1,), (1,)), ((), ())),
        precision=lax.Precision.HIGHEST,
        preferred_element_type=jnp.float32,
    )


def gaunt_density(density_matrix, gaunt_index, gaunt_value):
    harmonics = density_matrix.shape[0] // 2
    codes = jnp.arange(harmonics, dtype=jnp.int32)[:, None]
    first_table = (gaunt_index[0][None, :] == codes).astype(jnp.float32)
    second_table = (gaunt_index[1][None, :] == codes).astype(jnp.float32)
    target_table = (gaunt_index[2][None, :] == codes).astype(jnp.float32)
    collected = []
    for radial in range(2):
        for other in range(2):
            block = density_matrix[
                radial * harmonics : (radial + 1) * harmonics,
                other * harmonics : (other + 1) * harmonics,
            ]
            spread = jnp.dot(
                block,
                second_table,
                precision=lax.Precision.HIGHEST,
                preferred_element_type=jnp.float32,
            )
            picked = jnp.sum(spread * first_table, axis=0)
            collected.append(picked * gaunt_value)
    values = jnp.stack(collected)
    return lax.dot_general(
        values,
        target_table,
        (((1,), (1,)), ((), ())),
        precision=lax.Precision.HIGHEST,
        preferred_element_type=jnp.float32,
    )


def columns_of(ref, start, columns):
    return ref.at[:, pl.ds(pl.multiple_of(start, LANES), columns)]


def multiply(matching, pieces, out_ref):
    for at, (arrived, begin, end, vectors) in enumerate(pieces):
        arrived.wait()
        term = jnp.dot(matching[:, begin:end], vectors[begin:end, :], preferred_element_type=jnp.float32)
        if at == 0:
            out_ref[...] = term
        else:
            out_ref[...] += term


def fetch(source, target, sems, first, steps):
    depth = target.shape[0]
    pieces = []
    for step in range(steps):
        begin, end = depth * step // steps, depth * (step + 1) // steps
        copy = pltpu.make_async_copy(source.at[begin:end], target.at[begin:end], sems.at[first + step])
        copy.start()
        pieces.append((copy, begin, end, target))
    return pieces


def first_kernel(
    columns, own_ref, matching_hbm, vectors_hbm, leaving_ref, staying_ref, matching, vectors, vectors_a, sems
):
    own = own_ref[0]
    copy = pltpu.make_async_copy(matching_hbm, matching, sems.at[0])
    copy.start()
    leaving = fetch(columns_of(vectors_hbm, (1 - own) * columns, columns), vectors, sems, 1, LEAVING_STEPS)
    staying = fetch(
        columns_of(vectors_hbm, own * columns, columns // 2), vectors_a, sems, 1 + LEAVING_STEPS, STAYING_STEPS
    )
    copy.wait()
    multiply(matching, leaving, leaving_ref)
    multiply(matching, staying, staying_ref)


def second_kernel(columns, own_ref, matching, vectors_hbm, staying_ref, vectors, sems):
    start = own_ref[0] * columns + columns // 2
    multiply(matching, fetch(columns_of(vectors_hbm, start, columns // 2), vectors, sems, 0, LAST_STEPS), staying_ref)


VMEM = pl.BlockSpec(memory_space=pltpu.VMEM)
SMEM = pl.BlockSpec(memory_space=pltpu.SMEM)
HBM = pl.BlockSpec(memory_space=pltpu.HBM)


def cost(channels, depth, columns):
    return pl.CostEstimate(
        flops=2 * channels * depth * columns,
        bytes_accessed=2 * depth * (columns + channels) + 4 * channels * columns,
        transcendentals=0,
    )


def first_products(matching, vectors, own, columns):
    channels, depth = matching.shape
    return pl.pallas_call(
        functools.partial(first_kernel, columns),
        out_shape=(
            jax.ShapeDtypeStruct((channels, columns), jnp.float32),
            jax.ShapeDtypeStruct((channels, columns // 2), jnp.float32),
            jax.ShapeDtypeStruct(matching.shape, matching.dtype),
        ),
        in_specs=[SMEM, HBM, HBM],
        out_specs=(VMEM, VMEM, VMEM),
        scratch_shapes=[
            pltpu.VMEM((depth, columns), vectors.dtype),
            pltpu.VMEM((depth, columns // 2), vectors.dtype),
            pltpu.SemaphoreType.DMA((1 + LEAVING_STEPS + STAYING_STEPS,)),
        ],
        compiler_params=pltpu.CompilerParams(vmem_limit_bytes=VMEM_LIMIT),
        cost_estimate=cost(channels, depth, columns * 3 // 2),
        name="first_products",
    )(own.reshape(1), matching, vectors)


def second_products(matching, vectors, own, columns):
    channels, depth = matching.shape
    return pl.pallas_call(
        functools.partial(second_kernel, columns),
        out_shape=jax.ShapeDtypeStruct((channels, columns // 2), jnp.float32),
        in_specs=[SMEM, VMEM, HBM],
        out_specs=VMEM,
        scratch_shapes=[
            pltpu.VMEM((depth, columns // 2), vectors.dtype),
            pltpu.SemaphoreType.DMA((LAST_STEPS,)),
        ],
        compiler_params=pltpu.CompilerParams(vmem_limit_bytes=VMEM_LIMIT),
        cost_estimate=cost(channels, depth, columns // 2),
        name="second_products",
    )(own.reshape(1), matching, vectors)


def round_up(value, unit):
    return -(-value // unit) * unit


def tables_kernel(index_ref, value_ref, second_ref, first_ref, target_ref):
    entries = index_ref.shape[1]
    rows = lax.broadcasted_iota(jnp.int32, (LANES, entries), 0)
    hit = jnp.where(rows == index_ref[1:2, :], 1.0, 0.0).astype(jnp.bfloat16)
    second_ref[:LANES, :] = hit
    second_ref[LANES:, :] = hit
    first_rows = lax.broadcasted_iota(jnp.int32, (first_ref.shape[0], entries), 0)
    first_ref[...] = jnp.where(first_rows == index_ref[0:1, :], value_ref[...], 0.0)
    target_ref[...] = jnp.transpose(jnp.where(rows == index_ref[2:3, :], 1.0, 0.0)).astype(jnp.bfloat16)


def gaunt_tables(gaunt_index, gaunt_value, harmonics):
    entries = gaunt_value.shape[0]
    shapes = (
        jax.ShapeDtypeStruct((2 * LANES, entries), jnp.bfloat16),
        jax.ShapeDtypeStruct((round_up(harmonics, 8), entries), jnp.float32),
        jax.ShapeDtypeStruct((entries, LANES), jnp.bfloat16),
    )
    return pl.pallas_call(
        tables_kernel,
        out_shape=shapes,
        in_specs=[VMEM, VMEM],
        out_specs=(VMEM, VMEM, VMEM),
        compiler_params=pltpu.CompilerParams(vmem_limit_bytes=32 * 2**20),
        cost_estimate=pl.CostEstimate(flops=8 * 2**20, bytes_accessed=5 * 2**20, transcendentals=0),
        name="gaunt_tables",
    )(gaunt_index, gaunt_value.reshape(1, entries))


def two_parts(value):
    high = value.astype(jnp.bfloat16)
    return high, (value - high.astype(jnp.float32)).astype(jnp.bfloat16)


def finish_kernel(tile, top_ref, bottom_ref, second_ref, first_ref, target_ref, matrix_ref, density_ref, full):
    channels = matrix_ref.shape[0]
    harmonics = channels // 2
    extra = channels - LANES
    half = top_ref.shape[0]
    upper = jnp.concatenate([top_ref[...], bottom_ref[: LANES - half, :]], axis=0)
    rest = bottom_ref[LANES - half :, :]
    rows = lax.broadcasted_iota(jnp.int32, (LANES, LANES), 0)
    lanes = lax.broadcasted_iota(jnp.int32, (LANES, LANES), 1)
    corner_there = (rows < extra) & (lanes >= LANES // 2) & (lanes < LANES // 2 + extra)
    tall = jnp.concatenate([rest, jnp.zeros((LANES - rest.shape[0], LANES), jnp.float32)], axis=0)
    corner = pltpu.roll(upper, LANES // 2, 1)
    full[:LANES, :LANES] = jnp.where(corner_there, jnp.transpose(upper), upper)
    full[:LANES, LANES:] = jnp.transpose(tall)
    full[LANES:, :LANES] = jnp.zeros((full.shape[0] - LANES, LANES), jnp.float32)
    full[LANES : LANES + rest.shape[0], :LANES] = rest
    full[LANES:, LANES:] = jnp.zeros((full.shape[0] - LANES, LANES), jnp.float32)
    full[LANES:channels, LANES:] = corner[:extra]
    matrix_ref[...] = full[:channels, :channels]

    height = first_ref.shape[0]
    entries = second_ref.shape[1]
    blocks = []
    for radial in range(2):
        strip = full[radial * harmonics : radial * harmonics + height, :]
        blocks.append(strip[:, :LANES])
        blocks.append(pltpu.roll(strip, 2 * LANES - harmonics, 1)[:, :LANES])
    stacked = jnp.concatenate(two_parts(jnp.concatenate(blocks, axis=0)), axis=1)
    kept = []
    for start in range(0, entries, tile):
        columns = slice(start, start + tile)
        spread = jnp.dot(stacked, second_ref[:, columns], preferred_element_type=jnp.float32)
        picked = []
        for pair in range(4):
            partial_sum = jnp.zeros((8, tile), jnp.float32)
            for at in range(0, height, 8):
                here = spread[pair * height + at : pair * height + at + 8, :]
                partial_sum = partial_sum + here * first_ref[at : at + 8, columns]
            picked.append(partial_sum)
        kept.append(jnp.concatenate(two_parts(jnp.concatenate(picked, axis=0)), axis=0))
    total = jnp.dot(jnp.concatenate(kept, axis=1), target_ref[...], preferred_element_type=jnp.float32)
    for pair in range(4):
        both = total[8 * pair : 8 * pair + 8] + total[32 + 8 * pair : 40 + 8 * pair]
        density_ref[pair : pair + 1, :] = jnp.sum(both, axis=0, keepdims=True)[:, :harmonics]


def finish(top, bottom, tables, channels):
    second, first, target = tables
    entries = second.shape[1]
    harmonics = channels // 2
    tile = TILE if entries % TILE == 0 else entries
    return pl.pallas_call(
        functools.partial(finish_kernel, tile),
        out_shape=(
            jax.ShapeDtypeStruct((channels, channels), jnp.float32),
            jax.ShapeDtypeStruct((4, harmonics), jnp.float32),
        ),
        in_specs=[VMEM] * 5,
        out_specs=(VMEM, VMEM),
        scratch_shapes=[pltpu.VMEM((round_up(harmonics + first.shape[0], 16), 2 * LANES), jnp.float32)],
        compiler_params=pltpu.CompilerParams(vmem_limit_bytes=32 * 2**20),
        name="finish",
    )(top, bottom, second, first, target)


def pack(matrix):
    channels = matrix.shape[0]
    extra = channels - LANES
    half = LANES // 2
    corner = jnp.pad(matrix[LANES:, LANES:], ((0, channels - extra), (half, LANES - half - extra)))
    rows = lax.broadcasted_iota(jnp.int32, (channels, LANES), 0)
    lanes = lax.broadcasted_iota(jnp.int32, (channels, LANES), 1)
    there = (rows < extra) & (lanes >= half) & (lanes < half + extra)
    packed = jnp.where(there, corner, matrix[:, :LANES])
    height = round_up(channels, 16) // 2
    height = round_up(height, 8)
    return packed[:height], jnp.pad(packed[height:], ((0, 2 * height - channels), (0, 0)))


def plain_body(matching, vectors, weights, gaunt_index, gaunt_value):
    partial_value = jnp.dot(matching, vectors, preferred_element_type=jnp.float32)
    summed = lax.psum(partial_value, "basis")
    local_terms = weighted_pairs(summed, weights)
    density_matrix = lax.psum(local_terms, "band")
    return (density_matrix, gaunt_density(density_matrix, gaunt_index, gaunt_value))


def halves(block, bit):
    middle = block.shape[1] // 2
    low, high = block[:, :middle], block[:, middle:]
    return jnp.where(bit == 1, low, high), jnp.where(bit == 1, high, low)


def direct_sum(block, steps, exchange):
    arrived = [block]
    for which in range(1, 1 << len(steps)):
        mask = band_mask = 0
        for at, (on_basis, on_band) in enumerate(steps):
            if which >> at & 1:
                mask, band_mask = mask ^ on_basis, band_mask ^ on_band
        odd = mask.bit_count() & 1
        arrived.append(exchange(block, mask | odd, band_mask))
    while len(arrived) > 1:
        arrived = [first + second for first, second in zip(arrived[::2], arrived[1::2])]
    return arrived[0]


def body(basis, band, matching, vectors, weights, gaunt_index, gaunt_value):
    index = lax.axis_index("basis")
    levels = basis.bit_length() - 1
    channels, columns = matching.shape[0], vectors.shape[1]
    bits = [(index >> level) & 1 for level in range(levels)]
    own = functools.reduce(jnp.bitwise_xor, bits)

    def exchange(block, mask, band_mask=0):
        pairs = [
            (i * band + j, (i ^ mask) * band + (j ^ band_mask))
            for i in range(basis)
            for j in range(band)
        ]
        return lax.ppermute(block, ("basis", "band"), pairs)

    leaving, staying_a, matching = first_products(matching, vectors, own, columns // 2)
    arriving = exchange(leaving, 1)
    staying_b = second_products(matching, vectors, own, columns // 2)
    width = columns // 8
    low, high = staying_a + arriving[:, : 2 * width], staying_b + arriving[:, 2 * width :]

    def quarter(first, second):
        pair = jnp.where(first == 1, high, low)
        return jnp.where(second == 1, pair[:, width:], pair[:, :width])

    come_b = exchange(quarter(1 - bits[1], 1 - bits[2]), 6)
    come_x = exchange(quarter(1 - bits[1], bits[2]), 3)
    come_z = exchange(quarter(bits[1], 1 - bits[2]), 5)
    block = quarter(bits[1], bits[2]) + come_x + come_z + come_b
    for level in range(3, levels - 1):
        sent, kept = halves(block, bits[level])
        block = kept + exchange(sent, 1 | (1 << level))
    block, weights, gaunt_index, gaunt_value = lax.optimization_barrier((block, weights, gaunt_index, gaunt_value))
    come = exchange(block, 1 | (1 << (levels - 1)))
    tables = gaunt_tables(gaunt_index, gaunt_value, channels // 2)
    begin = own * (columns // 2) + (2 * bits[1] + bits[2]) * width
    block_weights = lax.dynamic_slice_in_dim(weights, begin, width)
    for level in range(3, levels - 1):
        middle = block_weights.shape[0] // 2
        block_weights = jnp.where(bits[level] == 1, block_weights[middle:], block_weights[:middle])
    come, tables, block_weights = lax.optimization_barrier((come, tables, block_weights))
    block = block + come

    top, bottom = pack(weighted_pairs(block, block_weights))
    which = own
    mine, rest = jnp.where(which == 1, bottom, top), jnp.where(which == 1, top, bottom)
    terms = mine + exchange(rest, 1)
    if band > 1:
        terms = terms + (exchange(mine, 0, 1) + exchange(rest, 1, 1))
    steps = [(0, 1 << level) for level in range(1, band.bit_length() - 1)]
    steps += [(1 << level, 0) for level in range(1, levels - 1)]
    for at in range(0, len(steps), GROUP):
        terms = direct_sum(terms, steps[at : at + GROUP], exchange)
    other = exchange(terms, 1)
    top = jnp.where(which == 1, other, terms)
    bottom = jnp.where(which == 1, terms, other)
    return finish(top, bottom, tables, channels)


def solution(mesh):
    basis, band = mesh.shape["basis"], mesh.shape["band"]

    def choose(*arrays):
        channels, depth = arrays[0].shape
        columns = arrays[1].shape[1]
        powers = basis & (basis - 1) == 0 and band & (band - 1) == 0 and basis >= 16
        sizes = columns % (16 * LANES) == 0 and depth % 256 == 0
        if powers and sizes and channels % 2 == 0 and LANES < channels <= LANES + LANES // 2:
            return body(basis, band, *arrays)
        return plain_body(*arrays)

    return jax.shard_map(
        choose,
        mesh=mesh,
        in_specs=(P(None, "basis"), P("basis", "band"), P("band"), P(), P()),
        out_specs=(P(), P()),
        check_vma=False,
    )
```

```python
import functools

import jax
import jax.numpy as jnp
from jax import lax
from jax.experimental import pallas as pl
from jax.experimental.pallas import tpu as pltpu
from jax.sharding import PartitionSpec as P

LANES = 128
SPILL_LOW, SPILL_HIGH = 48, 56
TILE = 1024
LEAVING_STEPS, STAYING_STEPS, LAST_STEPS = 2, 1, 2
GROUP = 2
VMEM_LIMIT = 52 * 2**20


def weighted_pairs(coeffs, band_weights):
    scaled = coeffs * band_weights[None, :]
    return lax.dot_general(
        scaled,
        coeffs,
        (((1,), (1,)), ((), ())),
        precision=lax.Precision.HIGHEST,
        preferred_element_type=jnp.float32,
    )


def gaunt_density(density_matrix, gaunt_index, gaunt_value):
    harmonics = density_matrix.shape[0] // 2
    codes = jnp.arange(harmonics, dtype=jnp.int32)[:, None]
    first_table = (gaunt_index[0][None, :] == codes).astype(jnp.float32)
    second_table = (gaunt_index[1][None, :] == codes).astype(jnp.float32)
    target_table = (gaunt_index[2][None, :] == codes).astype(jnp.float32)
    collected = []
    for radial in range(2):
        for other in range(2):
            block = density_matrix[
                radial * harmonics : (radial + 1) * harmonics,
                other * harmonics : (other + 1) * harmonics,
            ]
            spread = jnp.dot(
                block,
                second_table,
                precision=lax.Precision.HIGHEST,
                preferred_element_type=jnp.float32,
            )
            picked = jnp.sum(spread * first_table, axis=0)
            collected.append(picked * gaunt_value)
    values = jnp.stack(collected)
    return lax.dot_general(
        values,
        target_table,
        (((1,), (1,)), ((), ())),
        precision=lax.Precision.HIGHEST,
        preferred_element_type=jnp.float32,
    )


def columns_of(ref, start, columns):
    return ref.at[:, pl.ds(pl.multiple_of(start, LANES), columns)]


def multiply(matching, pieces, out_ref):
    for at, (arrived, begin, end, vectors) in enumerate(pieces):
        arrived.wait()
        term = jnp.dot(matching[:, begin:end], vectors[begin:end, :], preferred_element_type=jnp.float32)
        if at == 0:
            out_ref[...] = term
        else:
            out_ref[...] += term


def fetch(source, target, sems, first, steps):
    depth = target.shape[0]
    pieces = []
    for step in range(steps):
        begin, end = depth * step // steps, depth * (step + 1) // steps
        copy = pltpu.make_async_copy(source.at[begin:end], target.at[begin:end], sems.at[first + step])
        copy.start()
        pieces.append((copy, begin, end, target))
    return pieces


def first_kernel(
    columns, own_ref, matching_hbm, vectors_hbm, leaving_ref, staying_ref, matching, vectors, vectors_a, sems
):
    own = own_ref[0]
    copy = pltpu.make_async_copy(matching_hbm, matching, sems.at[0])
    copy.start()
    leaving = fetch(columns_of(vectors_hbm, (1 - own) * columns, columns), vectors, sems, 1, LEAVING_STEPS)
    staying = fetch(
        columns_of(vectors_hbm, own * columns, columns // 2), vectors_a, sems, 1 + LEAVING_STEPS, STAYING_STEPS
    )
    copy.wait()
    multiply(matching, leaving, leaving_ref)
    multiply(matching, staying, staying_ref)


def second_kernel(columns, own_ref, matching, vectors_hbm, staying_ref, vectors, sems):
    start = own_ref[0] * columns + columns // 2
    multiply(matching, fetch(columns_of(vectors_hbm, start, columns // 2), vectors, sems, 0, LAST_STEPS), staying_ref)


VMEM = pl.BlockSpec(memory_space=pltpu.VMEM)
SMEM = pl.BlockSpec(memory_space=pltpu.SMEM)
HBM = pl.BlockSpec(memory_space=pltpu.HBM)


def cost(channels, depth, columns):
    return pl.CostEstimate(
        flops=2 * channels * depth * columns,
        bytes_accessed=2 * depth * (columns + channels) + 4 * channels * columns,
        transcendentals=0,
    )


def first_products(matching, vectors, own, columns):
    channels, depth = matching.shape
    return pl.pallas_call(
        functools.partial(first_kernel, columns),
        out_shape=(
            jax.ShapeDtypeStruct((channels, columns), jnp.float32),
            jax.ShapeDtypeStruct((channels, columns // 2), jnp.float32),
            jax.ShapeDtypeStruct(matching.shape, matching.dtype),
        ),
        in_specs=[SMEM, HBM, HBM],
        out_specs=(VMEM, VMEM, VMEM),
        scratch_shapes=[
            pltpu.VMEM((depth, columns), vectors.dtype),
            pltpu.VMEM((depth, columns // 2), vectors.dtype),
            pltpu.SemaphoreType.DMA((1 + LEAVING_STEPS + STAYING_STEPS,)),
        ],
        compiler_params=pltpu.CompilerParams(vmem_limit_bytes=VMEM_LIMIT),
        cost_estimate=cost(channels, depth, columns * 3 // 2),
        name="first_products",
    )(own.reshape(1), matching, vectors)


def second_products(matching, vectors, own, columns):
    channels, depth = matching.shape
    return pl.pallas_call(
        functools.partial(second_kernel, columns),
        out_shape=jax.ShapeDtypeStruct((channels, columns // 2), jnp.float32),
        in_specs=[SMEM, VMEM, HBM],
        out_specs=VMEM,
        scratch_shapes=[
            pltpu.VMEM((depth, columns // 2), vectors.dtype),
            pltpu.SemaphoreType.DMA((LAST_STEPS,)),
        ],
        compiler_params=pltpu.CompilerParams(vmem_limit_bytes=VMEM_LIMIT),
        cost_estimate=cost(channels, depth, columns // 2),
        name="second_products",
    )(own.reshape(1), matching, vectors)


def round_up(value, unit):
    return -(-value // unit) * unit


def tables_kernel(index_ref, value_ref, second_ref, first_ref, target_ref):
    entries = index_ref.shape[1]
    rows = lax.broadcasted_iota(jnp.int32, (LANES, entries), 0)
    hit = jnp.where(rows == index_ref[1:2, :], 1.0, 0.0).astype(jnp.bfloat16)
    second_ref[:LANES, :] = hit
    second_ref[LANES:, :] = hit
    first_rows = lax.broadcasted_iota(jnp.int32, (first_ref.shape[0], entries), 0)
    first_ref[...] = jnp.where(first_rows == index_ref[0:1, :], value_ref[...], 0.0)
    target_ref[...] = jnp.transpose(jnp.where(rows == index_ref[2:3, :], 1.0, 0.0)).astype(jnp.bfloat16)


def gaunt_tables(gaunt_index, gaunt_value, harmonics):
    entries = gaunt_value.shape[0]
    shapes = (
        jax.ShapeDtypeStruct((2 * LANES, entries), jnp.bfloat16),
        jax.ShapeDtypeStruct((round_up(harmonics, 8), entries), jnp.float32),
        jax.ShapeDtypeStruct((entries, LANES), jnp.bfloat16),
    )
    return pl.pallas_call(
        tables_kernel,
        out_shape=shapes,
        in_specs=[VMEM, VMEM],
        out_specs=(VMEM, VMEM, VMEM),
        compiler_params=pltpu.CompilerParams(vmem_limit_bytes=32 * 2**20),
        cost_estimate=pl.CostEstimate(flops=8 * 2**20, bytes_accessed=5 * 2**20, transcendentals=0),
        name="gaunt_tables",
    )(gaunt_index, gaunt_value.reshape(1, entries))


def two_parts(value):
    high = value.astype(jnp.bfloat16)
    return high, (value - high.astype(jnp.float32)).astype(jnp.bfloat16)


def finish_kernel(tile, top_ref, bottom_ref, second_ref, first_ref, target_ref, matrix_ref, density_ref, full):
    channels = matrix_ref.shape[0]
    harmonics = channels // 2
    extra = channels - LANES
    half = top_ref.shape[0]
    spill = channels - 2 * half
    upper = jnp.concatenate([top_ref[...], bottom_ref[: LANES - half, :]], axis=0)
    rest = bottom_ref[LANES - half :, :]
    rows = lax.broadcasted_iota(jnp.int32, (LANES, LANES), 0)
    lanes = lax.broadcasted_iota(jnp.int32, (LANES, LANES), 1)
    borrowed = (rows < LANES // 2) & (lanes >= LANES // 2)
    turned = pltpu.roll(upper, LANES // 2, 1)
    last = jnp.where(lanes[:8] < LANES // 2, turned[SPILL_LOW : SPILL_LOW + 8], upper[SPILL_HIGH : SPILL_HIGH + 8])
    last = jnp.where(rows[:8] < spill, last, 0.0)
    blank = jnp.zeros((LANES - rest.shape[0] - 8, LANES), jnp.float32)
    tall = jnp.concatenate([rest, last, blank], axis=0)
    full[:LANES, :LANES] = jnp.where(borrowed, jnp.transpose(upper), upper)
    full[:LANES, LANES:] = jnp.transpose(tall)
    full[LANES:, :LANES] = tall[: full.shape[0] - LANES]
    full[LANES:, LANES:] = jnp.zeros((full.shape[0] - LANES, LANES), jnp.float32)
    full[LANES:channels, LANES:] = turned[:extra]
    matrix_ref[...] = full[:channels, :channels]

    height = first_ref.shape[0]
    entries = second_ref.shape[1]
    blocks = []
    for radial in range(2):
        strip = full[radial * harmonics : radial * harmonics + height, :]
        blocks.append(strip[:, :LANES])
        blocks.append(pltpu.roll(strip, 2 * LANES - harmonics, 1)[:, :LANES])
    stacked = jnp.concatenate(two_parts(jnp.concatenate(blocks, axis=0)), axis=1)
    kept = []
    for start in range(0, entries, tile):
        columns = slice(start, start + tile)
        spread = jnp.dot(stacked, second_ref[:, columns], preferred_element_type=jnp.float32)
        picked = []
        for pair in range(4):
            partial_sum = jnp.zeros((8, tile), jnp.float32)
            for at in range(0, height, 8):
                here = spread[pair * height + at : pair * height + at + 8, :]
                partial_sum = partial_sum + here * first_ref[at : at + 8, columns]
            picked.append(partial_sum)
        kept.append(jnp.concatenate(two_parts(jnp.concatenate(picked, axis=0)), axis=0))
    total = jnp.dot(jnp.concatenate(kept, axis=1), target_ref[...], preferred_element_type=jnp.float32)
    for pair in range(4):
        both = total[8 * pair : 8 * pair + 8] + total[32 + 8 * pair : 40 + 8 * pair]
        density_ref[pair : pair + 1, :] = jnp.sum(both, axis=0, keepdims=True)[:, :harmonics]


def finish(top, bottom, tables, channels):
    second, first, target = tables
    entries = second.shape[1]
    harmonics = channels // 2
    tile = TILE if entries % TILE == 0 else entries
    return pl.pallas_call(
        functools.partial(finish_kernel, tile),
        out_shape=(
            jax.ShapeDtypeStruct((channels, channels), jnp.float32),
            jax.ShapeDtypeStruct((4, harmonics), jnp.float32),
        ),
        in_specs=[VMEM] * 5,
        out_specs=(VMEM, VMEM),
        scratch_shapes=[pltpu.VMEM((round_up(harmonics + first.shape[0], 16), 2 * LANES), jnp.float32)],
        compiler_params=pltpu.CompilerParams(vmem_limit_bytes=32 * 2**20),
        name="finish",
    )(top, bottom, second, first, target)


def pack(matrix):
    channels = matrix.shape[0]
    half = LANES // 2
    height = channels // 16 * 8

    def placed(part, row, lane):
        sizes = ((row, 2 * height - row - part.shape[0]), (lane, LANES - lane - part.shape[1]))
        return jnp.pad(part, sizes)

    last = matrix[2 * height :, :LANES]
    moved = (
        placed(matrix[LANES:, LANES:], 0, half)
        + placed(last[:, :half], SPILL_LOW, half)
        + placed(last[:, half:], SPILL_HIGH, half)
    )
    rows = lax.broadcasted_iota(jnp.int32, moved.shape, 0)
    lanes = lax.broadcasted_iota(jnp.int32, moved.shape, 1)
    packed = jnp.where((rows < half) & (lanes >= half), moved, matrix[: 2 * height, :LANES])
    return packed[:height], packed[height:]


def plain_body(matching, vectors, weights, gaunt_index, gaunt_value):
    partial_value = jnp.dot(matching, vectors, preferred_element_type=jnp.float32)
    summed = lax.psum(partial_value, "basis")
    local_terms = weighted_pairs(summed, weights)
    density_matrix = lax.psum(local_terms, "band")
    return (density_matrix, gaunt_density(density_matrix, gaunt_index, gaunt_value))


def halves(block, bit):
    middle = block.shape[1] // 2
    low, high = block[:, :middle], block[:, middle:]
    return jnp.where(bit == 1, low, high), jnp.where(bit == 1, high, low)


def direct_sum(block, steps, exchange):
    arrived = [block]
    for which in range(1, 1 << len(steps)):
        mask = band_mask = 0
        for at, (on_basis, on_band) in enumerate(steps):
            if which >> at & 1:
                mask, band_mask = mask ^ on_basis, band_mask ^ on_band
        odd = mask.bit_count() & 1
        arrived.append(exchange(block, mask | odd, band_mask))
    while len(arrived) > 1:
        arrived = [first + second for first, second in zip(arrived[::2], arrived[1::2])]
    return arrived[0]


def body(basis, band, matching, vectors, weights, gaunt_index, gaunt_value):
    index = lax.axis_index("basis")
    levels = basis.bit_length() - 1
    channels, columns = matching.shape[0], vectors.shape[1]
    bits = [(index >> level) & 1 for level in range(levels)]
    own = functools.reduce(jnp.bitwise_xor, bits)

    def exchange(block, mask, band_mask=0):
        pairs = [
            (i * band + j, (i ^ mask) * band + (j ^ band_mask))
            for i in range(basis)
            for j in range(band)
        ]
        return lax.ppermute(block, ("basis", "band"), pairs)

    leaving, staying_a, matching = first_products(matching, vectors, own, columns // 2)
    arriving = exchange(leaving, 1)
    staying_b = second_products(matching, vectors, own, columns // 2)
    width = columns // 8
    low, high = staying_a + arriving[:, : 2 * width], staying_b + arriving[:, 2 * width :]

    def quarter(first, second):
        pair = jnp.where(first == 1, high, low)
        return jnp.where(second == 1, pair[:, width:], pair[:, :width])

    come_b = exchange(quarter(1 - bits[1], 1 - bits[2]), 6)
    come_x = exchange(quarter(1 - bits[1], bits[2]), 3)
    come_z = exchange(quarter(bits[1], 1 - bits[2]), 5)
    block = quarter(bits[1], bits[2]) + come_x + come_z + come_b
    for level in range(3, levels - 1):
        sent, kept = halves(block, bits[level])
        block = kept + exchange(sent, 1 | (1 << level))
    block, weights, gaunt_index, gaunt_value = lax.optimization_barrier((block, weights, gaunt_index, gaunt_value))
    come = exchange(block, 1 | (1 << (levels - 1)))
    tables = gaunt_tables(gaunt_index, gaunt_value, channels // 2)
    begin = own * (columns // 2) + (2 * bits[1] + bits[2]) * width
    block_weights = lax.dynamic_slice_in_dim(weights, begin, width)
    for level in range(3, levels - 1):
        middle = block_weights.shape[0] // 2
        block_weights = jnp.where(bits[level] == 1, block_weights[middle:], block_weights[:middle])
    come, tables, block_weights = lax.optimization_barrier((come, tables, block_weights))
    block = block + come

    top, bottom = pack(weighted_pairs(block, block_weights))
    which = own
    mine, rest = jnp.where(which == 1, bottom, top), jnp.where(which == 1, top, bottom)
    terms = mine + exchange(rest, 1)
    if band > 1:
        terms = terms + (exchange(mine, 0, 1) + exchange(rest, 1, 1))
    steps = [(0, 1 << level) for level in range(1, band.bit_length() - 1)]
    steps += [(1 << level, 0) for level in range(1, levels - 1)]
    for at in range(0, len(steps), GROUP):
        terms = direct_sum(terms, steps[at : at + GROUP], exchange)
    other = exchange(terms, 1)
    top = jnp.where(which == 1, other, terms)
    bottom = jnp.where(which == 1, terms, other)
    return finish(top, bottom, tables, channels)


def solution(mesh):
    basis, band = mesh.shape["basis"], mesh.shape["band"]

    def choose(*arrays):
        channels, depth = arrays[0].shape
        columns = arrays[1].shape[1]
        powers = basis & (basis - 1) == 0 and band & (band - 1) == 0 and basis >= 16
        sizes = columns % (16 * LANES) == 0 and depth % 256 == 0
        if powers and sizes and channels % 2 == 0 and LANES + 16 <= channels <= LANES + 40 and channels % 16 <= 8:
            return body(basis, band, *arrays)
        return plain_body(*arrays)

    return jax.shard_map(
        choose,
        mesh=mesh,
        in_specs=(P(None, "basis"), P("basis", "band"), P("band"), P(), P()),
        out_specs=(P(), P()),
        check_vma=False,
    )
```

```python
import functools

import jax
import jax.numpy as jnp
from jax import lax
from jax.experimental import pallas as pl
from jax.experimental.pallas import tpu as pltpu
from jax.sharding import PartitionSpec as P

LANES = 128
SPILL_LOW, SPILL_HIGH = 48, 56
TILE = 1024
LEAVING_STEPS, STAYING_STEPS, LAST_STEPS = 2, 2, 2
GROUP = 2
VMEM_LIMIT = 52 * 2**20


def weighted_pairs(coeffs, band_weights):
    scaled = coeffs * band_weights[None, :]
    return lax.dot_general(
        scaled,
        coeffs,
        (((1,), (1,)), ((), ())),
        precision=lax.Precision.HIGHEST,
        preferred_element_type=jnp.float32,
    )


def gaunt_density(density_matrix, gaunt_index, gaunt_value):
    harmonics = density_matrix.shape[0] // 2
    codes = jnp.arange(harmonics, dtype=jnp.int32)[:, None]
    first_table = (gaunt_index[0][None, :] == codes).astype(jnp.float32)
    second_table = (gaunt_index[1][None, :] == codes).astype(jnp.float32)
    target_table = (gaunt_index[2][None, :] == codes).astype(jnp.float32)
    collected = []
    for radial in range(2):
        for other in range(2):
            block = density_matrix[
                radial * harmonics : (radial + 1) * harmonics,
                other * harmonics : (other + 1) * harmonics,
            ]
            spread = jnp.dot(
                block,
                second_table,
                precision=lax.Precision.HIGHEST,
                preferred_element_type=jnp.float32,
            )
            picked = jnp.sum(spread * first_table, axis=0)
            collected.append(picked * gaunt_value)
    values = jnp.stack(collected)
    return lax.dot_general(
        values,
        target_table,
        (((1,), (1,)), ((), ())),
        precision=lax.Precision.HIGHEST,
        preferred_element_type=jnp.float32,
    )


def columns_of(ref, start, columns):
    return ref.at[:, pl.ds(pl.multiple_of(start, LANES), columns)]


def multiply(matching, pieces, out_ref):
    for at, (arrived, begin, end, vectors) in enumerate(pieces):
        arrived.wait()
        term = jnp.dot(matching[:, begin:end], vectors[begin:end, :], preferred_element_type=jnp.float32)
        if at == 0:
            out_ref[...] = term
        else:
            out_ref[...] += term


def fetch(source, target, sems, first, steps):
    depth = target.shape[0]
    pieces = []
    for step in range(steps):
        begin, end = depth * step // steps, depth * (step + 1) // steps
        copy = pltpu.make_async_copy(source.at[begin:end], target.at[begin:end], sems.at[first + step])
        copy.start()
        pieces.append((copy, begin, end, target))
    return pieces


def first_kernel(
    columns, own_ref, matching_hbm, vectors_hbm, leaving_ref, staying_ref, matching, vectors, vectors_a, sems
):
    own = own_ref[0]
    copy = pltpu.make_async_copy(matching_hbm, matching, sems.at[0])
    copy.start()
    leaving = fetch(columns_of(vectors_hbm, (1 - own) * columns, columns), vectors, sems, 1, LEAVING_STEPS)
    staying = fetch(
        columns_of(vectors_hbm, own * columns, columns // 2), vectors_a, sems, 1 + LEAVING_STEPS, STAYING_STEPS
    )
    copy.wait()
    multiply(matching, leaving, leaving_ref)
    multiply(matching, staying, staying_ref)


def second_kernel(columns, own_ref, matching, vectors_hbm, staying_ref, vectors, sems):
    start = own_ref[0] * columns + columns // 2
    multiply(matching, fetch(columns_of(vectors_hbm, start, columns // 2), vectors, sems, 0, LAST_STEPS), staying_ref)


VMEM = pl.BlockSpec(memory_space=pltpu.VMEM)
SMEM = pl.BlockSpec(memory_space=pltpu.SMEM)
HBM = pl.BlockSpec(memory_space=pltpu.HBM)


def cost(channels, depth, columns):
    return pl.CostEstimate(
        flops=2 * channels * depth * columns,
        bytes_accessed=2 * depth * (columns + channels) + 4 * channels * columns,
        transcendentals=0,
    )


def first_products(matching, vectors, own, columns):
    channels, depth = matching.shape
    return pl.pallas_call(
        functools.partial(first_kernel, columns),
        out_shape=(
            jax.ShapeDtypeStruct((channels, columns), jnp.float32),
            jax.ShapeDtypeStruct((channels, columns // 2), jnp.float32),
            jax.ShapeDtypeStruct(matching.shape, matching.dtype),
        ),
        in_specs=[SMEM, HBM, HBM],
        out_specs=(VMEM, VMEM, VMEM),
        scratch_shapes=[
            pltpu.VMEM((depth, columns), vectors.dtype),
            pltpu.VMEM((depth, columns // 2), vectors.dtype),
            pltpu.SemaphoreType.DMA((1 + LEAVING_STEPS + STAYING_STEPS,)),
        ],
        compiler_params=pltpu.CompilerParams(vmem_limit_bytes=VMEM_LIMIT),
        cost_estimate=cost(channels, depth, columns * 3 // 2),
        name="first_products",
    )(own.reshape(1), matching, vectors)


def second_products(matching, vectors, own, columns):
    channels, depth = matching.shape
    return pl.pallas_call(
        functools.partial(second_kernel, columns),
        out_shape=jax.ShapeDtypeStruct((channels, columns // 2), jnp.float32),
        in_specs=[SMEM, VMEM, HBM],
        out_specs=VMEM,
        scratch_shapes=[
            pltpu.VMEM((depth, columns // 2), vectors.dtype),
            pltpu.SemaphoreType.DMA((LAST_STEPS,)),
        ],
        compiler_params=pltpu.CompilerParams(vmem_limit_bytes=VMEM_LIMIT),
        cost_estimate=cost(channels, depth, columns // 2),
        name="second_products",
    )(own.reshape(1), matching, vectors)


def round_up(value, unit):
    return -(-value // unit) * unit


def tables_kernel(index_ref, value_ref, second_ref, first_ref, target_ref):
    entries = index_ref.shape[1]
    rows = lax.broadcasted_iota(jnp.int32, (LANES, entries), 0)
    hit = jnp.where(rows == index_ref[1:2, :], 1.0, 0.0).astype(jnp.bfloat16)
    second_ref[:LANES, :] = hit
    second_ref[LANES:, :] = hit
    first_rows = lax.broadcasted_iota(jnp.int32, (first_ref.shape[0], entries), 0)
    first_ref[...] = jnp.where(first_rows == index_ref[0:1, :], value_ref[...], 0.0)
    target_ref[...] = jnp.transpose(jnp.where(rows == index_ref[2:3, :], 1.0, 0.0)).astype(jnp.bfloat16)


def gaunt_tables(gaunt_index, gaunt_value, harmonics):
    entries = gaunt_value.shape[0]
    shapes = (
        jax.ShapeDtypeStruct((2 * LANES, entries), jnp.bfloat16),
        jax.ShapeDtypeStruct((round_up(harmonics, 8), entries), jnp.float32),
        jax.ShapeDtypeStruct((entries, LANES), jnp.bfloat16),
    )
    return pl.pallas_call(
        tables_kernel,
        out_shape=shapes,
        in_specs=[VMEM, VMEM],
        out_specs=(VMEM, VMEM, VMEM),
        compiler_params=pltpu.CompilerParams(vmem_limit_bytes=32 * 2**20),
        cost_estimate=pl.CostEstimate(flops=8 * 2**20, bytes_accessed=5 * 2**20, transcendentals=0),
        name="gaunt_tables",
    )(gaunt_index, gaunt_value.reshape(1, entries))


def two_parts(value):
    high = value.astype(jnp.bfloat16)
    return high, (value - high.astype(jnp.float32)).astype(jnp.bfloat16)


def finish_kernel(tile, top_ref, bottom_ref, second_ref, first_ref, target_ref, matrix_ref, density_ref, full):
    channels = matrix_ref.shape[0]
    harmonics = channels // 2
    extra = channels - LANES
    half = top_ref.shape[0]
    spill = channels - 2 * half
    upper = jnp.concatenate([top_ref[...], bottom_ref[: LANES - half, :]], axis=0)
    rest = bottom_ref[LANES - half :, :]
    rows = lax.broadcasted_iota(jnp.int32, (LANES, LANES), 0)
    lanes = lax.broadcasted_iota(jnp.int32, (LANES, LANES), 1)
    borrowed = (rows < LANES // 2) & (lanes >= LANES // 2)
    turned = pltpu.roll(upper, LANES // 2, 1)
    last = jnp.where(lanes[:8] < LANES // 2, turned[SPILL_LOW : SPILL_LOW + 8], upper[SPILL_HIGH : SPILL_HIGH + 8])
    last = jnp.where(rows[:8] < spill, last, 0.0)
    blank = jnp.zeros((LANES - rest.shape[0] - 8, LANES), jnp.float32)
    tall = jnp.concatenate([rest, last, blank], axis=0)
    full[:LANES, :LANES] = jnp.where(borrowed, jnp.transpose(upper), upper)
    full[:LANES, LANES:] = jnp.transpose(tall)
    full[LANES:, :LANES] = tall[: full.shape[0] - LANES]
    full[LANES:, LANES:] = jnp.zeros((full.shape[0] - LANES, LANES), jnp.float32)
    full[LANES:channels, LANES:] = turned[:extra]
    matrix_ref[...] = full[:channels, :channels]

    height = first_ref.shape[0]
    entries = second_ref.shape[1]
    blocks = []
    for radial in range(2):
        strip = full[radial * harmonics : radial * harmonics + height, :]
        blocks.append(strip[:, :LANES])
        blocks.append(pltpu.roll(strip, 2 * LANES - harmonics, 1)[:, :LANES])
    stacked = jnp.concatenate(two_parts(jnp.concatenate(blocks, axis=0)), axis=1)
    kept = []
    for start in range(0, entries, tile):
        columns = slice(start, start + tile)
        spread = jnp.dot(stacked, second_ref[:, columns], preferred_element_type=jnp.float32)
        picked = []
        for pair in range(4):
            partial_sum = jnp.zeros((8, tile), jnp.float32)
            for at in range(0, height, 8):
                here = spread[pair * height + at : pair * height + at + 8, :]
                partial_sum = partial_sum + here * first_ref[at : at + 8, columns]
            picked.append(partial_sum)
        kept.append(jnp.concatenate(two_parts(jnp.concatenate(picked, axis=0)), axis=0))
    total = jnp.dot(jnp.concatenate(kept, axis=1), target_ref[...], preferred_element_type=jnp.float32)
    for pair in range(4):
        both = total[8 * pair : 8 * pair + 8] + total[32 + 8 * pair : 40 + 8 * pair]
        density_ref[pair : pair + 1, :] = jnp.sum(both, axis=0, keepdims=True)[:, :harmonics]


def finish(top, bottom, tables, channels):
    second, first, target = tables
    entries = second.shape[1]
    harmonics = channels // 2
    tile = TILE if entries % TILE == 0 else entries
    return pl.pallas_call(
        functools.partial(finish_kernel, tile),
        out_shape=(
            jax.ShapeDtypeStruct((channels, channels), jnp.float32),
            jax.ShapeDtypeStruct((4, harmonics), jnp.float32),
        ),
        in_specs=[VMEM] * 5,
        out_specs=(VMEM, VMEM),
        scratch_shapes=[pltpu.VMEM((round_up(harmonics + first.shape[0], 16), 2 * LANES), jnp.float32)],
        compiler_params=pltpu.CompilerParams(vmem_limit_bytes=32 * 2**20),
        name="finish",
    )(top, bottom, second, first, target)


def pack(matrix):
    channels = matrix.shape[0]
    half = LANES // 2
    height = channels // 16 * 8

    def placed(part, row, lane):
        sizes = ((row, 2 * height - row - part.shape[0]), (lane, LANES - lane - part.shape[1]))
        return jnp.pad(part, sizes)

    last = matrix[2 * height :, :LANES]
    moved = (
        placed(matrix[LANES:, LANES:], 0, half)
        + placed(last[:, :half], SPILL_LOW, half)
        + placed(last[:, half:], SPILL_HIGH, half)
    )
    rows = lax.broadcasted_iota(jnp.int32, moved.shape, 0)
    lanes = lax.broadcasted_iota(jnp.int32, moved.shape, 1)
    packed = jnp.where((rows < half) & (lanes >= half), moved, matrix[: 2 * height, :LANES])
    return packed[:height], packed[height:]


def plain_body(matching, vectors, weights, gaunt_index, gaunt_value):
    partial_value = jnp.dot(matching, vectors, preferred_element_type=jnp.float32)
    summed = lax.psum(partial_value, "basis")
    local_terms = weighted_pairs(summed, weights)
    density_matrix = lax.psum(local_terms, "band")
    return (density_matrix, gaunt_density(density_matrix, gaunt_index, gaunt_value))


def halves(block, bit):
    middle = block.shape[1] // 2
    low, high = block[:, :middle], block[:, middle:]
    return jnp.where(bit == 1, low, high), jnp.where(bit == 1, high, low)


def direct_sum(block, steps, exchange):
    arrived = [block]
    for which in range(1, 1 << len(steps)):
        mask = band_mask = 0
        for at, (on_basis, on_band) in enumerate(steps):
            if which >> at & 1:
                mask, band_mask = mask ^ on_basis, band_mask ^ on_band
        odd = mask.bit_count() & 1
        arrived.append(exchange(block, mask | odd, band_mask))
    while len(arrived) > 1:
        arrived = [first + second for first, second in zip(arrived[::2], arrived[1::2])]
    return arrived[0]


def body(basis, band, matching, vectors, weights, gaunt_index, gaunt_value):
    index = lax.axis_index("basis")
    levels = basis.bit_length() - 1
    channels, columns = matching.shape[0], vectors.shape[1]
    bits = [(index >> level) & 1 for level in range(levels)]
    own = functools.reduce(jnp.bitwise_xor, bits)

    def exchange(block, mask, band_mask=0):
        pairs = [
            (i * band + j, (i ^ mask) * band + (j ^ band_mask))
            for i in range(basis)
            for j in range(band)
        ]
        return lax.ppermute(block, ("basis", "band"), pairs)

    leaving, staying_a, matching = first_products(matching, vectors, own, columns // 2)
    arriving = exchange(leaving, 1)
    staying_b = second_products(matching, vectors, own, columns // 2)
    width = columns // 8
    low, high = staying_a + arriving[:, : 2 * width], staying_b + arriving[:, 2 * width :]

    def quarter(first, second):
        pair = jnp.where(first == 1, high, low)
        return jnp.where(second == 1, pair[:, width:], pair[:, :width])

    come_b = exchange(quarter(1 - bits[1], 1 - bits[2]), 6)
    come_x = exchange(quarter(1 - bits[1], bits[2]), 3)
    come_z = exchange(quarter(bits[1], 1 - bits[2]), 5)
    block = quarter(bits[1], bits[2]) + come_x + come_z + come_b
    for level in range(3, levels - 1):
        sent, kept = halves(block, bits[level])
        block = kept + exchange(sent, 1 | (1 << level))
    block, weights, gaunt_index, gaunt_value = lax.optimization_barrier((block, weights, gaunt_index, gaunt_value))
    come = exchange(block, 1 | (1 << (levels - 1)))
    tables = gaunt_tables(gaunt_index, gaunt_value, channels // 2)
    begin = own * (columns // 2) + (2 * bits[1] + bits[2]) * width
    block_weights = lax.dynamic_slice_in_dim(weights, begin, width)
    for level in range(3, levels - 1):
        middle = block_weights.shape[0] // 2
        block_weights = jnp.where(bits[level] == 1, block_weights[middle:], block_weights[:middle])
    come, tables, block_weights = lax.optimization_barrier((come, tables, block_weights))
    block = block + come

    top, bottom = pack(weighted_pairs(block, block_weights))
    which = own
    mine, rest = jnp.where(which == 1, bottom, top), jnp.where(which == 1, top, bottom)
    terms = mine + exchange(rest, 1)
    if band > 1:
        terms = terms + (exchange(mine, 0, 1) + exchange(rest, 1, 1))
    steps = [(0, 1 << level) for level in range(1, band.bit_length() - 1)]
    steps += [(1 << level, 0) for level in range(1, levels - 1)]
    for at in range(0, len(steps), GROUP):
        terms = direct_sum(terms, steps[at : at + GROUP], exchange)
    other = exchange(terms, 1)
    top = jnp.where(which == 1, other, terms)
    bottom = jnp.where(which == 1, terms, other)
    return finish(top, bottom, tables, channels)


def solution(mesh):
    basis, band = mesh.shape["basis"], mesh.shape["band"]

    def choose(*arrays):
        channels, depth = arrays[0].shape
        columns = arrays[1].shape[1]
        powers = basis & (basis - 1) == 0 and band & (band - 1) == 0 and basis >= 16
        sizes = columns % (16 * LANES) == 0 and depth % 256 == 0
        if powers and sizes and channels % 2 == 0 and LANES + 16 <= channels <= LANES + 40 and channels % 16 <= 8:
            return body(basis, band, *arrays)
        return plain_body(*arrays)

    return jax.shard_map(
        choose,
        mesh=mesh,
        in_specs=(P(None, "basis"), P("basis", "band"), P("band"), P(), P()),
        out_specs=(P(), P()),
        check_vma=False,
    )
```
